32 devices in a mesh: sp: 8 (over y, x, core), ch: 4 (over z).
Axes of the slice: x: 2, y: 2, z: 4, core: 2. Of those that a mesh axis runs over, the one named last changes fastest.
Arguments:
- volume: bfloat16 [256, 16, 8, 128], P('ch', 'sp'), may hold values from -6 to 6
- filters: bfloat16 [256, 3, 3, 3, 256], P('ch'), may hold values from -0.078125 to 0.078125
- cotangent: bfloat16 [256, 16, 8, 128], P('ch', 'sp'), may hold values from -6 to 6
Outputs:
- response: bfloat16 [256, 16, 8, 128], P('ch', 'sp')
- input_grad: bfloat16 [256, 16, 8, 128], P('ch', 'sp')
- filter_grad: bfloat16 [256, 3, 3, 3, 256], P('ch')
The draws below stay inside these ranges and needn't reach their ends.
All inputs are finite; a program needn't handle non-finite values.
Results may differ from the reference program's by a relative error of at most 0.0024.
Values may be sent and summed in bfloat16 or wider, within the bound.
A program may use at most 64 MiB of HBM per device.

```python
import math
import jax
import jax.numpy as jnp
from jax import lax

C = 256
F = 256
HEIGHT = 8
WIDTH = 128
DEPTH = 16


def shard_levels(stream_key, shape, cuts, least, high):
    level, own = 1.0, jax.random.fold_in(stream_key, 6)
    for dim, blocks in cuts:
        heights = jnp.exp(jax.random.uniform(jax.random.fold_in(own, dim), (blocks,), jnp.float32, least / len(cuts), high / len(cuts)))
        level = level * jnp.repeat(heights, shape[dim] // blocks).reshape([-1 if axis == dim else 1 for axis in range(len(shape))])
    return level


def scatter_about(rng, shape, width, most, split=(), kind=jnp.bfloat16):
    entries = jax.random.normal(rng, shape, jnp.float32) * width
    if len(split) > 0:
        entries = shard_levels(rng, shape, split, -0.22, 0.18) * entries
    return jnp.clip(entries, min=-most, max=most).astype(kind)


def setup_inputs(seed: int = 0) -> dict:
    streams_of = jax.random.split(jax.random.key(seed), 4)
    volume = scatter_about(streams_of[0], (C, DEPTH, HEIGHT, WIDTH), 1.0, 6.0, ((0, 4), (1, 8)))
    filters = scatter_about(streams_of[1], (F, 3, 3, 3, C), (27 * C) ** -0.5, 0.078125, ((0, 4),))
    cotangent = scatter_about(streams_of[2], (F, DEPTH, HEIGHT, WIDTH), 1.0, 6.0, ((0, 4), (1, 8)))
    return {"volume": volume, "filters": filters, "cotangent": cotangent}


def convolve(field, kernel):
    result = lax.conv_general_dilated(field[None], kernel, (1, 1, 1), ((1, 1), (1, 1), (1, 1)), dimension_numbers=('NCDHW', 'DHWIO', 'NCDHW'), precision=lax.Precision.HIGHEST)
    return result[0]

def reference(volume, filters, cotangent):
    field = volume.astype(jnp.float32)
    kernel = jnp.transpose(filters.astype(jnp.float32), (1, 2, 3, 4, 0))
    response, pullback = jax.vjp(convolve, field, kernel)
    field_grad, kernel_grad = pullback(cotangent.astype(jnp.float32))
    factor = 1.0 / math.sqrt(DEPTH * HEIGHT * WIDTH)
    return (response.astype(jnp.bfloat16), field_grad.astype(jnp.bfloat16), (jnp.transpose(kernel_grad, (4, 0, 1, 2, 3)) * factor).astype(jnp.bfloat16))
```

```python
import functools
import math

import jax
import jax.numpy as jnp
from jax import lax
from jax.experimental import pallas as pl
from jax.experimental.pallas import tpu as pltpu
from jax.sharding import PartitionSpec as P

BF = jnp.bfloat16
F32 = jnp.float32


def shifts(x, width):
    wide = x.astype(F32)
    lane = lax.broadcasted_iota(jnp.int32, x.shape, 1) % width
    before = jnp.where(lane == 0, 0.0, pltpu.roll(wide, 1, 1)).astype(BF)
    after = jnp.where(lane == width - 1, 0.0, pltpu.roll(wide, x.shape[1] - 1, 1)).astype(BF)
    return before, after


def kernel(
    n, S, D, H, W, gpc, factor,
    vol, cot, wfwd, sendw,
    resp, igrad, fout,
    vall, call, edge, crim, racc, iacc, rbuf, ibuf, wsb, wst, fpart, rs1, rs2, fog,
    zs, zr, ws1, wr1, ws2, wr2, cs, cr, rims, rimr, f1s, f1r, f2s, f2r, a1s, a1r, a2s, a2r,
):
    i, s = lax.axis_index("ch"), lax.axis_index("sp")
    cb, cells = vol.shape
    fb = cot.shape[0]
    F = fb * n
    HW = H * W
    G = 3 * gpc
    half = S // 2
    m, e = s // 2, s % 2
    sib = m * 2 + 1 - e

    bar = pltpu.get_barrier_semaphore()
    for d in range(1, n):
        pl.semaphore_signal(bar, inc=1, device_id={"ch": (i + d) % n}, device_id_type=pl.DeviceIdType.MESH)
    for d in range(1, S):
        pl.semaphore_signal(bar, inc=1, device_id={"sp": (s + d) % S}, device_id_type=pl.DeviceIdType.MESH)
    pl.semaphore_wait(bar, n + S - 2)

    def remote(src, dst, ssem, rsem, dev):
        return pltpu.make_async_remote_copy(
            src_ref=src, dst_ref=dst, send_sem=ssem, recv_sem=rsem,
            device_id=dev, device_id_type=pl.DeviceIdType.MESH,
        )

    def rows(j, size):
        return pl.ds(pl.multiple_of(j * size, size), size)

    def zcopy(which, direction, t):
        buf, own = ((vall, vol), (call, cot))[which]
        size = own.shape[0]
        block = i - t if direction == 0 else i + t
        spot = buf.at[1, rows(block, size), :]
        src = own if t == 0 else spot
        to = i + 1 if direction == 0 else i - 1
        return remote(src, spot, zs.at[which, direction, t], zr.at[which, direction, t], {"ch": to})

    def zsends(direction, t):
        return (i < n - 1) & (i - t >= 0) if direction == 0 else (i > 0) & (i + t <= n - 1)

    def zrecvs(direction, t):
        return i - 1 - t >= 0 if direction == 0 else i + 1 + t <= n - 1

    def zstart(which, t):
        for direction in range(2):
            @pl.when(zsends(direction, t))
            def _():
                zcopy(which, direction, t).start()

    def zwait(which, t):
        buf, own = ((vall, vol), (call, cot))[which]
        size = own.shape[0]
        for direction in range(2):
            @pl.when(zrecvs(direction, t))
            def _():
                block = i - 1 - t if direction == 0 else i + 1 + t
                spot = buf.at[1, rows(block, size), :]
                remote(spot, spot, zs.at[which, direction, t], zr.at[which, direction, t], {"ch": (i + 1) % n}).wait_recv()

    def zshift(which, t):
        buf, own = ((vall, vol), (call, cot))[which]
        size = own.shape[0]
        for direction in range(2):
            @pl.when(zrecvs(direction, t))
            def _():
                block = i - 1 - t if direction == 0 else i + 1 + t
                place = rows(block, size)
                before, after = shifts(buf[1, place, :], W)
                buf[0, place, :] = before if which == 0 else after
                buf[2, place, :] = after if which == 0 else before

    def zfinish(which, t):
        for direction in range(2):
            @pl.when(zsends(direction, t))
            def _():
                zcopy(which, direction, t).wait_send()

    def crim_copy(up):
        plane = cot.at[:, (D - 1) * HW : D * HW] if up else cot.at[:, 0:HW]
        k = 0 if up else 1
        return remote(plane, crim.at[k], cs.at[k], cr.at[k], {"sp": s + 1 if up else s - 1})

    def rim_copy(which, up):
        acc, buf = ((racc, rbuf), (iacc, ibuf))[which]
        k = 0 if up else 1
        src = acc.at[D + 1 if up else 0, :, W : W + HW]
        return remote(src, buf.at[k], rims.at[which, k], rimr.at[which, k], {"sp": s + 1 if up else s - 1})

    def both_ways(act):
        @pl.when(s < S - 1)
        def _():
            act(True)

        @pl.when(s > 0)
        def _():
            act(False)

    carried = -(-G // S)

    def w1_copy(r, d):
        g = s + r * S
        return remote(
            sendw.at[(i + d) % n, g], wsb.at[g, rows(i, fb), :], ws1.at[r, d - 1], wr1.at[r, d - 1], {"ch": (i + d) % n}
        )

    def w2_copy(r, d, g):
        return remote(wsb.at[g], wsb.at[g], ws2.at[r, d - 1], wr2.at[r, d - 1], {"sp": (s + d) % S})

    def w_mine(act):
        for r in range(carried):
            @pl.when(s + r * S < G)
            def _():
                act(r, s + r * S)

    zstart(0, 0)
    both_ways(lambda up: crim_copy(up).start())

    def w1_go(r, g):
        for d in range(1, n):
            w1_copy(r, d).start()
        wsb[g, rows(i, fb), :] = sendw[i, g]

    w_mine(w1_go)

    x = vol[...]
    before, after = shifts(x, W)
    vall[0, rows(i, cb), :] = before
    vall[1, rows(i, cb), :] = x
    vall[2, rows(i, cb), :] = after
    x = cot[...]
    before, after = shifts(x, W)
    call[0, rows(i, fb), :] = after
    call[1, rows(i, fb), :] = x
    call[2, rows(i, fb), :] = before
    edge[...] = jnp.zeros_like(edge)
    for c, part in enumerate((after, x, before)):
        for z in range(D):
            edge[c, z + 1, :, W : W + HW] = part[:, z * HW : (z + 1) * HW]
    racc[...] = jnp.zeros_like(racc)
    iacc[...] = jnp.zeros_like(iacc)

    def w2_go(r, g):
        for d in range(1, n):
            w1_copy(r, d).wait()
        for d in range(1, S):
            w2_copy(r, d, g).start()

    def crim_use(up):
        pass

    def early():
        w_mine(w2_go)

        @pl.when(s > 0)
        def _():
            remote(crim.at[0], crim.at[0], cs.at[0], cr.at[0], {"sp": (s + 1) % S}).wait_recv()
            x = crim[0]
            before, after = shifts(x, W)
            for c, part in enumerate((after, x, before)):
                edge[c, 0, :, W : W + HW] = part

        @pl.when(s < S - 1)
        def _():
            remote(crim.at[1], crim.at[1], cs.at[1], cr.at[1], {"sp": (s + 1) % S}).wait_recv()
            x = crim[1]
            before, after = shifts(x, W)
            for c, part in enumerate((after, x, before)):
                edge[c, D + 1, :, W : W + HW] = part

    for t in range(n - 1):
        zwait(0, t)
        if t + 1 < n - 1:
            zstart(0, t + 1)
        if t + 1 >= n - 2:
            if t + 1 == max(n - 2, 1):
                zstart(1, 0)
        zshift(0, t)
        if t == 0:
            early()

    R = fpart.shape[2]

    def fgrad():
        def body(step, _):
            a, c = step // 3, step % 3
            total = jnp.zeros((3 * fb, n * cb), F32)
            for z in range(D):
                plane = z + 2 - a
                left = jnp.concatenate(
                    [edge[c, plane, :, (2 - b) * W : (2 - b) * W + HW] for b in range(3)], axis=0
                )
                total += lax.dot_general(
                    left, vall[1, :, z * HW : (z + 1) * HW], (((1,), (1,)), ((), ())), preferred_element_type=F32
                )
            fflat[pl.ds(pl.multiple_of(step * 3 * fb, 8), 3 * fb), :] = total
            return 0

        lax.fori_loop(0, 9, body, 0)

    fflat = fpart.reshape(2 * half * R, n * cb)
    if 27 * fb < 2 * half * R:
        fflat[27 * fb :, :] = jnp.zeros((2 * half * R - 27 * fb, n * cb), F32)
    fgrad()

    def f1_copy():
        return remote(fpart.at[1 - e], rs1, f1s, f1r, {"sp": sib})

    f1_copy().start()

    tile = 2 * W if H % 2 == 0 else W
    per_plane = HW // tile

    def conv(weights, source, acc, size, forward):
        def body(step, _):
            z, q = step // per_plane, step % per_plane
            lanes = pl.ds(pl.multiple_of(step * tile, W), tile)
            right = source[:, :, lanes].reshape(3 * source.shape[1], tile)
            product = jnp.dot(weights[...], right, preferred_element_type=F32)
            for a in range(3):
                plane = z + 2 - a if forward else z + a
                for b in range(3):
                    off = 2 - b if forward else b
                    spot = pl.ds(pl.multiple_of(q * tile + off * W, W), tile)
                    k = 3 * a + b
                    acc[plane, :, spot] += product[k * size : (k + 1) * size]
            return 0

        lax.fori_loop(0, D * per_plane, body, 0)

    def response():
        conv(wfwd, vall, racc, fb, True)
        both_ways(lambda up: rim_copy(0, up).start())

    def f2_copy(d):
        to = ((m + d) % half) * 2 + e
        return remote(fpart.at[e, (m + d) % half], rs2.at[d - 1], f2s.at[d - 1], f2r.at[d - 1], {"sp": to})

    def reduce_pair():
        f1_copy().wait()
        fpart[e] = fpart[e] + rs1[...]
        for d in range(1, half):
            f2_copy(d).start()

    def a1_copy(d):
        spot = fog.at[e, m]
        return remote(spot, spot, a1s.at[d - 1], a1r.at[d - 1], {"sp": ((m + d) % half) * 2 + e})

    def a2_copy(d):
        spot = fog.at[e, (m - d + half) % half]
        return remote(spot, spot, a2s.at[d], a2r.at[d], {"sp": sib})

    def reduce_chips():
        total = fpart[e, m]
        for d in range(1, half):
            f2_copy(d).wait()
            total = total + rs2[d - 1]
        fog[e, m] = (total * factor).astype(BF)
        for d in range(1, half):
            a1_copy(d).start()
        a2_copy(0).start()

    def kernel_swapped():
        for r in range(carried):
            for d in range(1, S):
                g = (s - d + S) % S + r * S

                @pl.when(g < G)
                def _():
                    w2_copy(r, d, g).wait_recv()

        for c in range(3):
            for g in range(gpc):
                wst[g * W : (g + 1) * W, c * F : (c + 1) * F] = wsb[c * gpc + g].T

    def finish(which, out, acc, buf):
        @pl.when(s > 0)
        def _():
            remote(buf.at[0], buf.at[0], rims.at[which, 0], rimr.at[which, 0], {"sp": (s + 1) % S}).wait_recv()
            acc[1, :, W : W + HW] += buf[0]

        @pl.when(s < S - 1)
        def _():
            remote(buf.at[1], buf.at[1], rims.at[which, 1], rimr.at[which, 1], {"sp": (s + 1) % S}).wait_recv()
            acc[D, :, W : W + HW] += buf[1]

        for z in range(D):
            out[:, z * HW : (z + 1) * HW] = acc[z + 1, :, W : W + HW].astype(BF)

    def gather_forward():
        for d in range(1, half):
            a1_copy(d).wait_recv()
            a2_copy(d).start()

    work = [[response, kernel_swapped], [reduce_pair], [reduce_chips]]
    at = {}
    for k, items in enumerate(work):
        at.setdefault(min(k, max(n - 2, 0)), []).extend(items)
    for t in range(n - 1):
        zwait(1, t)
        if t + 1 < n - 1:
            zstart(1, t + 1)
        zshift(1, t)
        if t < n - 2:
            for item in at.get(t, []):
                item()
    for item in at.get(n - 2, []):
        if item is not reduce_chips:
            item()

    conv(wst, call, iacc, cb, False)
    both_ways(lambda up: rim_copy(1, up).start())
    reduce_chips()
    finish(0, resp, racc, rbuf)
    gather_forward()
    finish(1, igrad, iacc, ibuf)
    for d in range(half):
        spot = fog.at[1 - e, (m - d + half) % half]
        remote(spot, spot, a2s.at[d], a2r.at[d], {"sp": sib}).wait_recv()
    fout[...] = fog[...]

    for which in range(2):
        for t in range(n - 1):
            zfinish(which, t)
        both_ways(lambda up: rim_copy(which, up).wait_send())
    both_ways(lambda up: crim_copy(up).wait_send())

    def w2_end(r, g):
        for d in range(1, S):
            w2_copy(r, d, g).wait_send()

    w_mine(w2_end)
    for d in range(1, half):
        a1_copy(d).wait_send()
    for d in range(half):
        a2_copy(d).wait_send()


def local(n, S, volume, filters, cotangent):
    cb, D, H, W = volume.shape
    fb = cotangent.shape[0]
    C, F = cb * n, fb * n
    cells = D * H * W
    gpc = -(-9 * cb // W)
    G = 3 * gpc
    half = S // 2
    R = -(-27 * fb // (S * 16)) * 16
    factor = 1.0 / math.sqrt(cells * S)
    taps = filters.reshape(fb, 9, 3, C)
    wfwd = jnp.transpose(taps, (1, 0, 2, 3)).reshape(9 * fb, 3 * C)
    sendw = jnp.transpose(taps.reshape(fb, 9, 3, n, cb), (3, 2, 0, 1, 4)).reshape(n, 3, fb, 9 * cb)
    sendw = jnp.pad(sendw, ((0, 0), (0, 0), (0, 0), (0, gpc * W - 9 * cb)))
    sendw = jnp.transpose(sendw.reshape(n, 3, fb, gpc, W), (0, 1, 3, 2, 4)).reshape(n, G, fb, W)
    dma = pltpu.SemaphoreType.DMA
    spec = pl.BlockSpec(memory_space=pltpu.VMEM)
    carried = -(-G // S)
    pads = (H + 2) * W
    resp, igrad, fgrad = pl.pallas_call(
        functools.partial(kernel, n, S, D, H, W, gpc, factor),
        out_shape=(
            jax.ShapeDtypeStruct((fb, cells), BF),
            jax.ShapeDtypeStruct((cb, cells), BF),
            jax.ShapeDtypeStruct((2, half, R, C), BF),
        ),
        in_specs=[spec] * 4,
        out_specs=(spec,) * 3,
        scratch_shapes=[
            pltpu.VMEM((3, C, cells), BF),
            pltpu.VMEM((3, F, cells), BF),
            pltpu.VMEM((3, D + 2, fb, pads), BF),
            pltpu.VMEM((2, fb, H * W), BF),
            pltpu.VMEM((D + 2, fb, pads), F32),
            pltpu.VMEM((D + 2, cb, pads), F32),
            pltpu.VMEM((2, fb, H * W), F32),
            pltpu.VMEM((2, cb, H * W), F32),
            pltpu.VMEM((G, F, W), BF),
            pltpu.VMEM((gpc * W, 3 * F), BF),
            pltpu.VMEM((2, half, R, C), F32),
            pltpu.VMEM((half, R, C), F32),
            pltpu.VMEM((half - 1, R, C), F32),
            pltpu.VMEM((2, half, R, C), BF),
            dma((2, 2, n - 1)),
            dma((2, 2, n - 1)),
            dma((carried, n - 1)),
            dma((carried, n - 1)),
            dma((carried, S - 1)),
            dma((carried, S - 1)),
            dma((2,)),
            dma((2,)),
            dma((2, 2)),
            dma((2, 2)),
            dma,
            dma,
            dma((half - 1,)),
            dma((half - 1,)),
            dma((half - 1,)),
            dma((half - 1,)),
            dma((half,)),
            dma((half,)),
        ],
        compiler_params=pltpu.CompilerParams(
            collective_id=0, has_side_effects=True, vmem_limit_bytes=50 * 2**20
        ),
    )(volume.reshape(cb, cells), cotangent.reshape(fb, cells), wfwd, sendw)
    fgrad = fgrad.reshape(S * R, C)[: 27 * fb].reshape(3, 3, 3, fb, C)
    return (
        resp.reshape(fb, D, H, W),
        igrad.reshape(cb, D, H, W),
        jnp.transpose(fgrad, (3, 0, 2, 1, 4)),
    )


def solution(mesh):
    n, S = mesh.shape["ch"], mesh.shape["sp"]
    wide = P("ch", "sp", None, None)
    kern = P("ch", None, None, None, None)
    return jax.shard_map(
        functools.partial(local, n, S),
        mesh=mesh,
        in_specs=(wide, kern, wide),
        out_specs=(wide, wide, kern),
        check_vma=False,
    )
```

```python
import functools
import math

import jax
import jax.numpy as jnp
from jax import lax
from jax.experimental import pallas as pl
from jax.experimental.pallas import tpu as pltpu
from jax.sharding import PartitionSpec as P

BF = jnp.bfloat16
F32 = jnp.float32


def shifts(x, width):
    wide = x.astype(F32)
    lane = lax.broadcasted_iota(jnp.int32, x.shape, 1) % width
    before = jnp.where(lane == 0, 0.0, pltpu.roll(wide, 1, 1)).astype(BF)
    after = jnp.where(lane == width - 1, 0.0, pltpu.roll(wide, x.shape[1] - 1, 1)).astype(BF)
    return before, after


def kernel(
    n, S, D, H, W, gpc, factor,
    vol, cot, filt,
    resp, igrad, fout,
    vall, call, edge, crim, racc, iacc, rbuf, ibuf, wfwd, swb, wsb, wst, fpart, rs1, rs2, fog,
    zs, zr, ws1, wr1, ws2, wr2, cs, cr, rims, rimr, f1s, f1r, f2s, f2r, a1s, a1r, a2s, a2r,
):
    i, s = lax.axis_index("ch"), lax.axis_index("sp")
    cb, cells = vol.shape
    fb = cot.shape[0]
    F = fb * n
    HW = H * W
    G = 3 * gpc
    half = S // 2
    m, e = s // 2, s % 2
    sib = m * 2 + 1 - e

    bar = pltpu.get_barrier_semaphore()
    for d in range(1, n):
        pl.semaphore_signal(bar, inc=1, device_id={"ch": (i + d) % n}, device_id_type=pl.DeviceIdType.MESH)
    for d in range(1, S):
        pl.semaphore_signal(bar, inc=1, device_id={"sp": (s + d) % S}, device_id_type=pl.DeviceIdType.MESH)
    pl.semaphore_wait(bar, n + S - 2)

    def remote(src, dst, ssem, rsem, dev):
        return pltpu.make_async_remote_copy(
            src_ref=src, dst_ref=dst, send_sem=ssem, recv_sem=rsem,
            device_id=dev, device_id_type=pl.DeviceIdType.MESH,
        )

    def rows(j, size):
        return pl.ds(pl.multiple_of(j * size, size), size)

    def zcopy(which, direction, t):
        buf, own = ((vall, vol), (call, cot))[which]
        size = own.shape[0]
        block = i - t if direction == 0 else i + t
        spot = buf.at[1, rows(block, size), :]
        src = own if t == 0 else spot
        to = i + 1 if direction == 0 else i - 1
        return remote(src, spot, zs.at[which, direction, t], zr.at[which, direction, t], {"ch": to})

    def zsends(direction, t):
        return (i < n - 1) & (i - t >= 0) if direction == 0 else (i > 0) & (i + t <= n - 1)

    def zrecvs(direction, t):
        return i - 1 - t >= 0 if direction == 0 else i + 1 + t <= n - 1

    def zstart(which, t):
        for direction in range(2):
            @pl.when(zsends(direction, t))
            def _():
                zcopy(which, direction, t).start()

    def zwait(which, t):
        buf, own = ((vall, vol), (call, cot))[which]
        size = own.shape[0]
        for direction in range(2):
            @pl.when(zrecvs(direction, t))
            def _():
                block = i - 1 - t if direction == 0 else i + 1 + t
                spot = buf.at[1, rows(block, size), :]
                remote(spot, spot, zs.at[which, direction, t], zr.at[which, direction, t], {"ch": (i + 1) % n}).wait_recv()

    def zshift(which, t):
        buf, own = ((vall, vol), (call, cot))[which]
        size = own.shape[0]
        for direction in range(2):
            @pl.when(zrecvs(direction, t))
            def _():
                block = i - 1 - t if direction == 0 else i + 1 + t
                place = rows(block, size)
                before, after = shifts(buf[1, place, :], W)
                buf[0, place, :] = before if which == 0 else after
                buf[2, place, :] = after if which == 0 else before

    def zfinish(which, t):
        for direction in range(2):
            @pl.when(zsends(direction, t))
            def _():
                zcopy(which, direction, t).wait_send()

    def crim_copy(up):
        plane = cot.at[:, (D - 1) * HW : D * HW] if up else cot.at[:, 0:HW]
        k = 0 if up else 1
        return remote(plane, crim.at[k], cs.at[k], cr.at[k], {"sp": s + 1 if up else s - 1})

    def rim_copy(which, up):
        acc, buf = ((racc, rbuf), (iacc, ibuf))[which]
        k = 0 if up else 1
        src = acc.at[D + 1 if up else 0, :, W : W + HW]
        return remote(src, buf.at[k], rims.at[which, k], rimr.at[which, k], {"sp": s + 1 if up else s - 1})

    def both_ways(act):
        @pl.when(s < S - 1)
        def _():
            act(True)

        @pl.when(s > 0)
        def _():
            act(False)

    carried = -(-G // S)

    def w1_copy(r, d):
        g = s + r * S
        return remote(
            swb.at[r, (i + d) % n], wsb.at[g, rows(i, fb), :], ws1.at[r, d - 1], wr1.at[r, d - 1], {"ch": (i + d) % n}
        )

    def w2_copy(r, d, g):
        return remote(wsb.at[g], wsb.at[g], ws2.at[r, d - 1], wr2.at[r, d - 1], {"sp": (s + d) % S})

    def w_mine(act):
        for r in range(carried):
            @pl.when(s + r * S < G)
            def _():
                act(r, s + r * S)

    zstart(0, 0)
    both_ways(lambda up: crim_copy(up).start())

    tpg = W // cb

    def w1_go(r, g):
        c, q = g // gpc, g % gpc
        taps = [filt[jnp.minimum(q * tpg + u, 8) * 3 + c] for u in range(tpg)]
        for j in range(n):
            swb[r, j] = jnp.concatenate([tap[:, j * cb : (j + 1) * cb] for tap in taps], axis=1)
        for d in range(1, n):
            w1_copy(r, d).start()
        wsb[g, rows(i, fb), :] = swb[r, i]

    w_mine(w1_go)

    x = vol[...]
    before, after = shifts(x, W)
    vall[0, rows(i, cb), :] = before
    vall[1, rows(i, cb), :] = x
    vall[2, rows(i, cb), :] = after
    x = cot[...]
    before, after = shifts(x, W)
    call[0, rows(i, fb), :] = after
    call[1, rows(i, fb), :] = x
    call[2, rows(i, fb), :] = before
    edge[...] = jnp.zeros_like(edge)
    for c, part in enumerate((after, x, before)):
        for z in range(D):
            edge[c, z + 1, :, W : W + HW] = part[:, z * HW : (z + 1) * HW]
    for k in range(9):
        for c in range(3):
            wfwd[k * fb : (k + 1) * fb, c * cb * n : (c + 1) * cb * n] = filt[3 * k + c]
    racc[...] = jnp.zeros_like(racc)
    iacc[...] = jnp.zeros_like(iacc)

    def w2_go(r, g):
        for d in range(1, n):
            w1_copy(r, d).wait()
        for d in range(1, S):
            w2_copy(r, d, g).start()

    def early():
        w_mine(w2_go)

        @pl.when(s > 0)
        def _():
            remote(crim.at[0], crim.at[0], cs.at[0], cr.at[0], {"sp": (s + 1) % S}).wait_recv()
            x = crim[0]
            before, after = shifts(x, W)
            for c, part in enumerate((after, x, before)):
                edge[c, 0, :, W : W + HW] = part

        @pl.when(s < S - 1)
        def _():
            remote(crim.at[1], crim.at[1], cs.at[1], cr.at[1], {"sp": (s + 1) % S}).wait_recv()
            x = crim[1]
            before, after = shifts(x, W)
            for c, part in enumerate((after, x, before)):
                edge[c, D + 1, :, W : W + HW] = part

    for t in range(n - 1):
        zwait(0, t)
        if t + 1 < n - 1:
            zstart(0, t + 1)
        if t + 1 >= n - 2:
            if t + 1 == max(n - 2, 1):
                zstart(1, 0)
        zshift(0, t)
        if t == 0:
            early()

    R = fpart.shape[2]

    def fgrad():
        def body(step, _):
            a, c = step // 3, step % 3
            total = jnp.zeros((3 * fb, n * cb), F32)
            for z in range(D):
                plane = z + 2 - a
                left = jnp.concatenate(
                    [edge[c, plane, :, (2 - b) * W : (2 - b) * W + HW] for b in range(3)], axis=0
                )
                total += lax.dot_general(
                    left, vall[1, :, z * HW : (z + 1) * HW], (((1,), (1,)), ((), ())), preferred_element_type=F32
                )
            for b in range(3):
                fflat[rows(9 * a + 3 * b + c, fb), :] = total[b * fb : (b + 1) * fb]
            return 0

        lax.fori_loop(0, 9, body, 0)

    fflat = fpart.reshape(2 * half * R, n * cb)
    if 27 * fb < 2 * half * R:
        fflat[27 * fb :, :] = jnp.zeros((2 * half * R - 27 * fb, n * cb), F32)
    fgrad()

    def f1_copy():
        return remote(fpart.at[1 - e], rs1, f1s, f1r, {"sp": sib})

    f1_copy().start()

    tile = 2 * W if H % 2 == 0 else W
    per_plane = HW // tile

    def conv(weights, pick, acc, size, forward, part):
        for z in range(D):
            rim = ([0] if z == 0 else []) + ([2] if z == D - 1 else [])
            if forward:
                rim = [2 - a for a in rim]
            taps = {"all": [0, 1, 2], "rim": rim, "rest": [a for a in range(3) if a not in rim]}[part]
            if not taps:
                continue
            low, high = min(taps), max(taps) + 1

            def body(q, _):
                lanes = pl.ds(pl.multiple_of(z * HW + q * tile, W), tile)
                right = pick(lanes)
                left = weights(pl.ds(low * 3 * size, (high - low) * 3 * size))
                product = jnp.dot(left, right, preferred_element_type=F32)
                for a in taps:
                    plane = z + 2 - a if forward else z + a
                    for b in range(3):
                        off = 2 - b if forward else b
                        spot = pl.ds(pl.multiple_of(q * tile + off * W, W), tile)
                        k = 3 * (a - low) + b
                        acc[plane, :, spot] += product[k * size : (k + 1) * size]
                return 0

            lax.fori_loop(0, per_plane, body, 0)

    def response():
        conv(
            lambda r: wfwd[r, :], lambda lanes: vall[:, :, lanes].reshape(3 * cb * n, tile), racc, fb, True, "all"
        )
        both_ways(lambda up: rim_copy(0, up).start())

    def f2_copy(d):
        to = ((m + d) % half) * 2 + e
        return remote(fpart.at[e, (m + d) % half], rs2.at[d - 1], f2s.at[d - 1], f2r.at[d - 1], {"sp": to})

    def reduce_pair():
        f1_copy().wait()
        fpart[e] = fpart[e] + rs1[...]
        for d in range(1, half):
            f2_copy(d).start()

    def a1_copy(d):
        spot = fog.at[e, m]
        return remote(spot, spot, a1s.at[d - 1], a1r.at[d - 1], {"sp": ((m + d) % half) * 2 + e})

    def a2_copy(d):
        spot = fog.at[e, (m - d + half) % half]
        return remote(spot, spot, a2s.at[d], a2r.at[d], {"sp": sib})

    def reduce_chips():
        total = fpart[e, m]
        for d in range(1, half):
            f2_copy(d).wait()
            total = total + rs2[d - 1]
        fog[e, m] = (total * factor).astype(BF)
        for d in range(1, half):
            a1_copy(d).start()
        a2_copy(0).start()

    def kernel_swapped():
        for r in range(carried):
            for d in range(1, S):
                g = (s - d + S) % S + r * S

                @pl.when(g < G)
                def _():
                    w2_copy(r, d, g).wait_recv()

        def turn(j, _):
            for g in range(gpc):
                piece = jnp.concatenate([wsb[c * gpc + g, rows(j, fb), :] for c in range(3)], axis=0)
                wst[j, g * W : (g + 1) * W, :] = piece.T
            return 0

        lax.fori_loop(0, n, turn, 0)

    def conv_block(block, part="all"):
        conv(
            lambda r: wst[block, r, :],
            lambda lanes: call[:, rows(block, fb), lanes].reshape(3 * fb, tile),
            iacc, cb, False, part,
        )

    def conv_arrived(t, part="all"):
        for direction in range(2):
            @pl.when(zrecvs(direction, t))
            def _():
                conv_block(i - 1 - t if direction == 0 else i + 1 + t, part)

    def finish(which, out, acc, buf):
        @pl.when(s > 0)
        def _():
            remote(buf.at[0], buf.at[0], rims.at[which, 0], rimr.at[which, 0], {"sp": (s + 1) % S}).wait_recv()
            acc[1, :, W : W + HW] += buf[0]

        @pl.when(s < S - 1)
        def _():
            remote(buf.at[1], buf.at[1], rims.at[which, 1], rimr.at[which, 1], {"sp": (s + 1) % S}).wait_recv()
            acc[D, :, W : W + HW] += buf[1]

        for z in range(D):
            out[:, z * HW : (z + 1) * HW] = acc[z + 1, :, W : W + HW].astype(BF)

    def gather_forward():
        for d in range(1, half):
            a1_copy(d).wait_recv()
            a2_copy(d).start()

    kernel_swapped()
    conv_block(i)
    reduce_pair()
    last = n - 2
    for t in range(n - 1):
        zwait(1, t)
        if t < last:
            zstart(1, t + 1)
        zshift(1, t)
        if t < last:
            conv_arrived(t)
        if t == 0:
            response()
        if t == min(1, last):
            reduce_chips()
    conv_arrived(last, "rim")
    both_ways(lambda up: rim_copy(1, up).start())
    conv_arrived(last, "rest")
    finish(0, resp, racc, rbuf)
    gather_forward()
    finish(1, igrad, iacc, ibuf)
    for d in range(half):
        spot = fog.at[1 - e, (m - d + half) % half]
        remote(spot, spot, a2s.at[d], a2r.at[d], {"sp": sib}).wait_recv()
    fout[...] = fog.reshape(2 * half * R, n * cb)[0 : 27 * fb, :]

    for which in range(2):
        for t in range(n - 1):
            zfinish(which, t)
        both_ways(lambda up: rim_copy(which, up).wait_send())
    both_ways(lambda up: crim_copy(up).wait_send())

    def w2_end(r, g):
        for d in range(1, S):
            w2_copy(r, d, g).wait_send()

    w_mine(w2_end)
    for d in range(1, half):
        a1_copy(d).wait_send()
    for d in range(half):
        a2_copy(d).wait_send()


def local(n, S, volume, filters, cotangent):
    cb, D, H, W = volume.shape
    fb = cotangent.shape[0]
    C, F = cb * n, fb * n
    cells = D * H * W
    gpc = -(-9 // (W // cb))
    G = 3 * gpc
    half = S // 2
    R = -(-27 * fb // (S * 16)) * 16
    factor = 1.0 / math.sqrt(cells * S)
    filt = jnp.transpose(filters, (1, 2, 3, 0, 4)).reshape(27, fb, C)
    dma = pltpu.SemaphoreType.DMA
    spec = pl.BlockSpec(memory_space=pltpu.VMEM)
    carried = -(-G // S)
    pads = (H + 2) * W
    resp, igrad, fgrad = pl.pallas_call(
        functools.partial(kernel, n, S, D, H, W, gpc, factor),
        out_shape=(
            jax.ShapeDtypeStruct((fb, cells), BF),
            jax.ShapeDtypeStruct((cb, cells), BF),
            jax.ShapeDtypeStruct((27 * fb, C), BF),
        ),
        in_specs=[spec] * 3,
        out_specs=(spec,) * 3,
        scratch_shapes=[
            pltpu.VMEM((3, C, cells), BF),
            pltpu.VMEM((3, F, cells), BF),
            pltpu.VMEM((3, D + 2, fb, pads), BF),
            pltpu.VMEM((2, fb, H * W), BF),
            pltpu.VMEM((D + 2, fb, pads), F32),
            pltpu.VMEM((D + 2, cb, pads), F32),
            pltpu.VMEM((2, fb, H * W), F32),
            pltpu.VMEM((2, cb, H * W), F32),
            pltpu.VMEM((9 * fb, 3 * C), BF),
            pltpu.VMEM((carried, n, fb, W), BF),
            pltpu.VMEM((G, F, W), BF),
            pltpu.VMEM((n, gpc * W, 3 * fb), BF),
            pltpu.VMEM((2, half, R, C), F32),
            pltpu.VMEM((half, R, C), F32),
            pltpu.VMEM((half - 1, R, C), F32),
            pltpu.VMEM((2, half, R, C), BF),
            dma((2, 2, n - 1)),
            dma((2, 2, n - 1)),
            dma((carried, n - 1)),
            dma((carried, n - 1)),
            dma((carried, S - 1)),
            dma((carried, S - 1)),
            dma((2,)),
            dma((2,)),
            dma((2, 2)),
            dma((2, 2)),
            dma,
            dma,
            dma((half - 1,)),
            dma((half - 1,)),
            dma((half - 1,)),
            dma((half - 1,)),
            dma((half,)),
            dma((half,)),
        ],
        compiler_params=pltpu.CompilerParams(
            collective_id=0, has_side_effects=True, vmem_limit_bytes=50 * 2**20
        ),
    )(volume.reshape(cb, cells), cotangent.reshape(fb, cells), filt)
    return (
        resp.reshape(fb, D, H, W),
        igrad.reshape(cb, D, H, W),
        jnp.transpose(fgrad.reshape(3, 3, 3, fb, C), (3, 0, 1, 2, 4)),
    )


def solution(mesh):
    n, S = mesh.shape["ch"], mesh.shape["sp"]
    wide = P("ch", "sp", None, None)
    kern = P("ch", None, None, None, None)
    return jax.shard_map(
        functools.partial(local, n, S),
        mesh=mesh,
        in_specs=(wide, kern, wide),
        out_specs=(wide, wide, kern),
        check_vma=False,
    )
```

```python
import functools
import math

import jax
import jax.numpy as jnp
from jax import lax
from jax.experimental import pallas as pl
from jax.experimental.pallas import tpu as pltpu
from jax.sharding import PartitionSpec as P

BF = jnp.bfloat16
F32 = jnp.float32


def shifts(x, width):
    lane = lax.broadcasted_iota(jnp.int32, (x.shape[0], width), 1)
    first, last = lane == 0, lane == width - 1
    before, after = [], []
    for k in range(x.shape[1] // width):
        wide = x[:, k * width : (k + 1) * width].astype(F32)
        before.append(jnp.where(first, 0.0, pltpu.roll(wide, 1, 1)).astype(BF))
        after.append(jnp.where(last, 0.0, pltpu.roll(wide, width - 1, 1)).astype(BF))
    return jnp.concatenate(before, axis=1), jnp.concatenate(after, axis=1)


def kernel(
    n, S, D, H, W, gpc, factor,
    vol, cot, filt,
    resp, igrad, fout,
    vall, call, edge, crim, racc, iacc, rbuf, ibuf, wfwd, swb, wsb, wst, wl, lv, lc, lrim, lcall, fpart, rs1, rs2, fog,
    zs, zr, ws1, wr1, ws2, wr2, cs, cr, rims, rimr, f1s, f1r, f2s, f2r, a1s, a1r, a2s, a2r, ls, lr,
):
    i, s = lax.axis_index("ch"), lax.axis_index("sp")
    cb, cells = vol.shape
    fb = cot.shape[0]
    F = fb * n
    HW = H * W
    G = 3 * gpc
    half = S // 2
    m, e = s // 2, s % 2
    sib = m * 2 + 1 - e

    bar = pltpu.get_barrier_semaphore()
    for d in range(1, n):
        pl.semaphore_signal(bar, inc=1, device_id={"ch": (i + d) % n}, device_id_type=pl.DeviceIdType.MESH)
    for d in range(1, S):
        pl.semaphore_signal(bar, inc=1, device_id={"sp": (s + d) % S}, device_id_type=pl.DeviceIdType.MESH)
    pl.semaphore_wait(bar, n + S - 2)

    def remote(src, dst, ssem, rsem, dev):
        return pltpu.make_async_remote_copy(
            src_ref=src, dst_ref=dst, send_sem=ssem, recv_sem=rsem,
            device_id=dev, device_id_type=pl.DeviceIdType.MESH,
        )

    def rows(j, size):
        return pl.ds(pl.multiple_of(j * size, size), size)

    def zcopy(which, direction, t):
        land, own = ((lv, vol), (lc, cot))[which]
        block = i - t if direction == 0 else i + t
        src = own if t == 0 else land.at[block]
        to = i + 1 if direction == 0 else i - 1
        return remote(src, land.at[block], zs.at[which, direction, t], zr.at[which, direction, t], {"ch": to})

    def zsends(direction, t):
        return (i < n - 1) & (i - t >= 0) if direction == 0 else (i > 0) & (i + t <= n - 1)

    def zrecvs(direction, t):
        return i - 1 - t >= 0 if direction == 0 else i + 1 + t <= n - 1

    def zstart(which, t):
        for direction in range(2):
            @pl.when(zsends(direction, t))
            def _():
                zcopy(which, direction, t).start()

    def zwait(which, t):
        land = (lv, lc)[which]
        for direction in range(2):
            @pl.when(zrecvs(direction, t))
            def _():
                spot = land.at[i - 1 - t if direction == 0 else i + 1 + t]
                remote(spot, spot, zs.at[which, direction, t], zr.at[which, direction, t], {"ch": (i + 1) % n}).wait_recv()

    def zshift(which, t):
        land, buf = ((lv, vall), (lc, call))[which]
        size = land.shape[1]
        for direction in range(2):
            @pl.when(zrecvs(direction, t))
            def _():
                block = i - 1 - t if direction == 0 else i + 1 + t
                place = rows(block, size)
                x = land[block]
                before, after = shifts(x, W)
                buf[0, place, :] = before if which == 0 else after
                buf[1, place, :] = x
                buf[2, place, :] = after if which == 0 else before

    def zfinish(which, t):
        for direction in range(2):
            @pl.when(zsends(direction, t))
            def _():
                zcopy(which, direction, t).wait_send()

    def crim_copy(up):
        plane = cot.at[:, (D - 1) * HW : D * HW] if up else cot.at[:, 0:HW]
        k = 0 if up else 1
        return remote(plane, crim.at[k], cs.at[k], cr.at[k], {"sp": s + 1 if up else s - 1})

    def rim_copy(which, up):
        acc, buf = ((racc, rbuf), (iacc, ibuf))[which]
        k = 0 if up else 1
        src = acc.at[D + 1 if up else 0, :, W : W + HW]
        return remote(src, buf.at[k], rims.at[which, k], rimr.at[which, k], {"sp": s + 1 if up else s - 1})

    def both_ways(act):
        @pl.when(s < S - 1)
        def _():
            act(True)

        @pl.when(s > 0)
        def _():
            act(False)

    carried = -(-G // S)

    def w1_copy(r, d):
        g = s + r * S
        return remote(
            swb.at[r, (i + d) % n], wsb.at[g, rows(i, fb), :], ws1.at[r, d - 1], wr1.at[r, d - 1], {"ch": (i + d) % n}
        )

    def w2_copy(r, d, g):
        return remote(wsb.at[g], wsb.at[g], ws2.at[r, d - 1], wr2.at[r, d - 1], {"sp": (s + d) % S})

    def w_mine(act):
        for r in range(carried):
            @pl.when(s + r * S < G)
            def _():
                act(r, s + r * S)

    zstart(0, 0)
    both_ways(lambda up: crim_copy(up).start())

    tpg = W // cb

    def w1_go(r, g):
        c, q = g // gpc, g % gpc
        taps = [filt[jnp.minimum(q * tpg + u, 8) * 3 + c] for u in range(tpg)]
        for j in range(n):
            swb[r, j] = jnp.concatenate([tap[:, j * cb : (j + 1) * cb] for tap in taps], axis=1)
        for d in range(1, n):
            w1_copy(r, d).start()
        wsb[g, rows(i, fb), :] = swb[r, i]

    w_mine(w1_go)

    x = vol[...]
    before, after = shifts(x, W)
    vall[0, rows(i, cb), :] = before
    vall[1, rows(i, cb), :] = x
    vall[2, rows(i, cb), :] = after
    x = cot[...]
    before, after = shifts(x, W)
    call[0, rows(i, fb), :] = after
    call[1, rows(i, fb), :] = x
    call[2, rows(i, fb), :] = before
    ends = (i == 0) | (i == n - 1)
    far = jnp.where(i == 0, n - 1, 0)

    @pl.when(ends)
    def _():
        for c in range(3):
            call[c, rows(far, fb), :] = jnp.zeros((fb, cells), BF)

    edge[...] = jnp.zeros_like(edge)
    for c, part in enumerate((after, x, before)):
        for z in range(D):
            edge[c, z + 1, :, W : W + HW] = part[:, z * HW : (z + 1) * HW]
    for k in range(9):
        for c in range(3):
            wfwd[k * fb : (k + 1) * fb, c * cb * n : (c + 1) * cb * n] = filt[3 * k + c]
    racc[...] = jnp.zeros_like(racc)
    iacc[...] = jnp.zeros_like(iacc)

    def w2_go(r, g):
        for d in range(1, n):
            w1_copy(r, d).wait()
        for d in range(1, S):
            w2_copy(r, d, g).start()

    def early():
        w_mine(w2_go)

        @pl.when(s > 0)
        def _():
            remote(crim.at[0], crim.at[0], cs.at[0], cr.at[0], {"sp": (s + 1) % S}).wait_recv()
            x = crim[0]
            before, after = shifts(x, W)
            for c, part in enumerate((after, x, before)):
                edge[c, 0, :, W : W + HW] = part

        @pl.when(s < S - 1)
        def _():
            remote(crim.at[1], crim.at[1], cs.at[1], cr.at[1], {"sp": (s + 1) % S}).wait_recv()
            x = crim[1]
            before, after = shifts(x, W)
            for c, part in enumerate((after, x, before)):
                edge[c, D + 1, :, W : W + HW] = part

    for t in range(n - 1):
        zwait(0, t)
        if t + 1 < n - 1:
            zstart(0, t + 1)
        if t + 1 >= n - 2:
            if t + 1 == max(n - 2, 1):
                zstart(1, 0)
        zshift(0, t)
        if t == 0:
            early()

    R = fpart.shape[2]

    def fgrad():
        def body(a, _):
            total = jnp.zeros((9 * fb, n * cb), F32)
            for z in range(D):
                plane = z + 2 - a
                left = jnp.concatenate(
                    [edge[c, plane, :, (2 - b) * W : (2 - b) * W + HW] for b in range(3) for c in range(3)], axis=0
                )
                total += lax.dot_general(
                    left, vall[1, :, z * HW : (z + 1) * HW], (((1,), (1,)), ((), ())), preferred_element_type=F32
                )
            fflat[rows(a, 9 * fb), :] = total
            return 0

        lax.fori_loop(0, 3, body, 0)

    fflat = fpart.reshape(2 * half * R, n * cb)
    if 27 * fb < 2 * half * R:
        fflat[27 * fb :, :] = jnp.zeros((2 * half * R - 27 * fb, n * cb), F32)
    fgrad()

    def f1_copy():
        return remote(fpart.at[1 - e], rs1, f1s, f1r, {"sp": sib})

    f1_copy().start()

    tile = 4 * W if H % 4 == 0 else W
    per_plane = HW // tile

    def conv(weights, pick, acc, size, forward, part):
        for z in range(D):
            rim = ([0] if z == 0 else []) + ([2] if z == D - 1 else [])
            if forward:
                rim = [2 - a for a in rim]
            taps = {"all": [0, 1, 2], "rim": rim, "rest": [a for a in range(3) if a not in rim]}[part]
            if not taps:
                continue
            low, high = min(taps), max(taps) + 1

            def body(q, _):
                lanes = pl.ds(pl.multiple_of(z * HW + q * tile, W), tile)
                right = pick(lanes)
                left = weights(pl.ds(low * 3 * size, (high - low) * 3 * size))
                product = jnp.dot(left, right, preferred_element_type=F32)
                for a in taps:
                    plane = z + 2 - a if forward else z + a
                    for b in range(3):
                        off = 2 - b if forward else b
                        spot = pl.ds(pl.multiple_of(q * tile + off * W, W), tile)
                        k = 3 * (a - low) + b
                        acc[plane, :, spot] += product[k * size : (k + 1) * size]
                return 0

            lax.fori_loop(0, per_plane, body, 0)

    def response():
        conv(
            lambda r: wfwd[r, :], lambda lanes: vall[:, :, lanes].reshape(3 * cb * n, tile), racc, fb, True, "all"
        )
        both_ways(lambda up: rim_copy(0, up).start())

    def f2_copy(d):
        to = ((m + d) % half) * 2 + e
        return remote(fpart.at[e, (m + d) % half], rs2.at[d - 1], f2s.at[d - 1], f2r.at[d - 1], {"sp": to})

    def reduce_pair():
        f1_copy().wait()
        fpart[e] = fpart[e] + rs1[...]
        for d in range(1, half):
            f2_copy(d).start()

    def a1_copy(d):
        spot = fog.at[e, m]
        return remote(spot, spot, a1s.at[d - 1], a1r.at[d - 1], {"sp": ((m + d) % half) * 2 + e})

    def a2_copy(d):
        spot = fog.at[e, (m - d + half) % half]
        return remote(spot, spot, a2s.at[d], a2r.at[d], {"sp": sib})

    def reduce_chips():
        total = fpart[e, m]
        for d in range(1, half):
            f2_copy(d).wait()
            total = total + rs2[d - 1]
        fog[e, m] = (total * factor).astype(BF)
        for d in range(1, half):
            a1_copy(d).start()
        a2_copy(0).start()

    def kernel_swapped():
        for r in range(carried):
            for d in range(1, S):
                g = (s - d + S) % S + r * S

                @pl.when(g < G)
                def _():
                    w2_copy(r, d, g).wait_recv()

        for g in range(gpc):
            for c in range(3):
                wst[g * W : (g + 1) * W, c * F : (c + 1) * F] = wsb[c * gpc + g].T
            piece = jnp.concatenate([wsb[c * gpc + g, rows(far, fb), :] for c in range(3)], axis=0)
            wl[g * W : (g + 1) * W, :] = piece.T

    def most_blocks():
        conv(
            lambda r: wst[r, :], lambda lanes: call[:, :, lanes].reshape(3 * F, tile), iacc, cb, False, "all"
        )
        both_ways(lambda up: rim_copy(1, up).start())

    def far_rim(up):
        plane = lc.at[far, :, (D - 1) * HW : D * HW] if up else lc.at[far, :, 0:HW]
        k = 0 if up else 1
        return remote(plane, lrim.at[k], ls.at[k], lr.at[k], {"sp": s + 1 if up else s - 1})

    def far_use(k):
        remote(lrim.at[k], lrim.at[k], ls.at[k], lr.at[k], {"sp": (s + 1) % S}).wait_recv()
        x = lrim[k]
        before, after = shifts(x, W)
        right = jnp.concatenate([after, x, before], axis=0)
        a = 2 if k == 0 else 0
        product = jnp.dot(wl[3 * a * cb : 3 * (a + 1) * cb, :], right, preferred_element_type=F32)
        plane = 1 if k == 0 else D
        for b in range(3):
            iacc[plane, :, b * W : b * W + HW] += product[b * cb : (b + 1) * cb]

    def far_block():
        both_ways(lambda up: far_rim(up).start())
        x = lc[far]
        before, after = shifts(x, W)
        lcall[0:fb, :] = after
        lcall[fb : 2 * fb, :] = x
        lcall[2 * fb :, :] = before
        conv(lambda r: wl[r, :], lambda lanes: lcall[:, lanes], iacc, cb, False, "rest")

        @pl.when(s > 0)
        def _():
            far_use(0)

        @pl.when(s < S - 1)
        def _():
            far_use(1)

        both_ways(lambda up: far_rim(up).wait_send())

    def finish(which, out, acc, buf):
        @pl.when(s > 0)
        def _():
            remote(buf.at[0], buf.at[0], rims.at[which, 0], rimr.at[which, 0], {"sp": (s + 1) % S}).wait_recv()
            acc[1, :, W : W + HW] += buf[0]

        @pl.when(s < S - 1)
        def _():
            remote(buf.at[1], buf.at[1], rims.at[which, 1], rimr.at[which, 1], {"sp": (s + 1) % S}).wait_recv()
            acc[D, :, W : W + HW] += buf[1]

        for z in range(D):
            out[:, z * HW : (z + 1) * HW] = acc[z + 1, :, W : W + HW].astype(BF)

    def gather_forward():
        for d in range(1, half):
            a1_copy(d).wait_recv()
            a2_copy(d).start()

    last = n - 2
    for t in range(last):
        zwait(1, t)
        zstart(1, t + 1)
        if t == 0:
            response()
            reduce_pair()
        zshift(1, t)
    kernel_swapped()
    most_blocks()
    reduce_chips()
    finish(0, resp, racc, rbuf)
    gather_forward()
    zwait(1, last)

    @pl.when(ends)
    def _():
        far_block()

    finish(1, igrad, iacc, ibuf)
    for d in range(half):
        spot = fog.at[1 - e, (m - d + half) % half]
        remote(spot, spot, a2s.at[d], a2r.at[d], {"sp": sib}).wait_recv()
    fout[...] = fog.reshape(2 * half * R, n * cb)[0 : 27 * fb, :]

    for which in range(2):
        for t in range(n - 1):
            zfinish(which, t)
        both_ways(lambda up: rim_copy(which, up).wait_send())
    both_ways(lambda up: crim_copy(up).wait_send())

    def w2_end(r, g):
        for d in range(1, S):
            w2_copy(r, d, g).wait_send()

    w_mine(w2_end)
    for d in range(1, half):
        a1_copy(d).wait_send()
    for d in range(half):
        a2_copy(d).wait_send()


def local(n, S, volume, filters, cotangent):
    cb, D, H, W = volume.shape
    fb = cotangent.shape[0]
    C, F = cb * n, fb * n
    cells = D * H * W
    gpc = -(-9 // (W // cb))
    G = 3 * gpc
    half = S // 2
    R = -(-27 * fb // (S * 16)) * 16
    factor = 1.0 / math.sqrt(cells * S)
    filt = jnp.transpose(filters, (1, 2, 3, 0, 4)).reshape(27, fb, C)
    dma = pltpu.SemaphoreType.DMA
    spec = pl.BlockSpec(memory_space=pltpu.VMEM)
    carried = -(-G // S)
    pads = (H + 2) * W
    resp, igrad, fgrad = pl.pallas_call(
        functools.partial(kernel, n, S, D, H, W, gpc, factor),
        out_shape=(
            jax.ShapeDtypeStruct((fb, cells), BF),
            jax.ShapeDtypeStruct((cb, cells), BF),
            jax.ShapeDtypeStruct((27 * fb, C), BF),
        ),
        in_specs=[spec] * 3,
        out_specs=(spec,) * 3,
        scratch_shapes=[
            pltpu.VMEM((3, C, cells), BF),
            pltpu.VMEM((3, F, cells), BF),
            pltpu.VMEM((3, D + 2, fb, pads), BF),
            pltpu.VMEM((2, fb, H * W), BF),
            pltpu.VMEM((D + 2, fb, pads), F32),
            pltpu.VMEM((D + 2, cb, pads), F32),
            pltpu.VMEM((2, fb, H * W), F32),
            pltpu.VMEM((2, cb, H * W), F32),
            pltpu.VMEM((9 * fb, 3 * C), BF),
            pltpu.VMEM((carried, n, fb, W), BF),
            pltpu.VMEM((G, F, W), BF),
            pltpu.VMEM((gpc * W, 3 * F), BF),
            pltpu.VMEM((gpc * W, 3 * fb), BF),
            pltpu.VMEM((n, cb, cells), BF),
            pltpu.VMEM((n, fb, cells), BF),
            pltpu.VMEM((2, fb, H * W), BF),
            pltpu.VMEM((3 * fb, cells), BF),
            pltpu.VMEM((2, half, R, C), F32),
            pltpu.VMEM((half, R, C), F32),
            pltpu.VMEM((half - 1, R, C), F32),
            pltpu.VMEM((2, half, R, C), BF),
            dma((2, 2, n - 1)),
            dma((2, 2, n - 1)),
            dma((carried, n - 1)),
            dma((carried, n - 1)),
            dma((carried, S - 1)),
            dma((carried, S - 1)),
            dma((2,)),
            dma((2,)),
            dma((2, 2)),
            dma((2, 2)),
            dma,
            dma,
            dma((half - 1,)),
            dma((half - 1,)),
            dma((half - 1,)),
            dma((half - 1,)),
            dma((half,)),
            dma((half,)),
            dma((2,)),
            dma((2,)),
        ],
        compiler_params=pltpu.CompilerParams(
            collective_id=0, has_side_effects=True, vmem_limit_bytes=50 * 2**20
        ),
    )(volume.reshape(cb, cells), cotangent.reshape(fb, cells), filt)
    return (
        resp.reshape(fb, D, H, W),
        igrad.reshape(cb, D, H, W),
        jnp.transpose(fgrad.reshape(3, 3, 3, fb, C), (3, 0, 1, 2, 4)),
    )


def solution(mesh):
    n, S = mesh.shape["ch"], mesh.shape["sp"]
    wide = P("ch", "sp", None, None)
    kern = P("ch", None, None, None, None)
    return jax.shard_map(
        functools.partial(local, n, S),
        mesh=mesh,
        in_specs=(wide, kern, wide),
        out_specs=(wide, wide, kern),
        check_vma=False,
    )
```

```python
import functools
import math

import jax
import jax.numpy as jnp
from jax import lax
from jax.experimental import pallas as pl
from jax.experimental.pallas import tpu as pltpu
from jax.sharding import PartitionSpec as P

BF = jnp.bfloat16
F32 = jnp.float32


def shifts(x, width):
    lane = lax.broadcasted_iota(jnp.int32, (x.shape[0], width), 1)
    first, last = lane == 0, lane == width - 1
    before, after = [], []
    for k in range(x.shape[1] // width):
        wide = x[:, k * width : (k + 1) * width].astype(F32)
        before.append(jnp.where(first, 0.0, pltpu.roll(wide, 1, 1)).astype(BF))
        after.append(jnp.where(last, 0.0, pltpu.roll(wide, width - 1, 1)).astype(BF))
    return jnp.concatenate(before, axis=1), jnp.concatenate(after, axis=1)


def kernel(
    n, S, D, H, W, gpc, factor,
    vol, cot, filt,
    resp, igrad, fout,
    vall, call, edge, crim, racc, iacc, rbuf, ibuf, wfwd, swb, wsb, wst, wl, lv, lc, lrim, lcall, fpart, rs1, rs2, fog,
    zs, zr, ws1, wr1, ws2, wr2, cs, cr, rims, rimr, f1s, f1r, f2s, f2r, a1s, a1r, a2s, a2r, ls, lr, ws3, wr3,
):
    i, s = lax.axis_index("ch"), lax.axis_index("sp")
    cb, cells = vol.shape
    fb = cot.shape[0]
    F = fb * n
    HW = H * W
    G = 3 * gpc
    half = S // 2
    m, e = s // 2, s % 2
    sib = m * 2 + 1 - e

    bar = pltpu.get_barrier_semaphore()
    for d in range(1, n):
        pl.semaphore_signal(bar, inc=1, device_id={"ch": (i + d) % n}, device_id_type=pl.DeviceIdType.MESH)
    for d in range(1, S):
        pl.semaphore_signal(bar, inc=1, device_id={"sp": (s + d) % S}, device_id_type=pl.DeviceIdType.MESH)
    pl.semaphore_wait(bar, n + S - 2)

    def remote(src, dst, ssem, rsem, dev):
        return pltpu.make_async_remote_copy(
            src_ref=src, dst_ref=dst, send_sem=ssem, recv_sem=rsem,
            device_id=dev, device_id_type=pl.DeviceIdType.MESH,
        )

    def rows(j, size):
        return pl.ds(pl.multiple_of(j * size, size), size)

    def zcopy(which, direction, t):
        land, own = ((lv, vol), (lc, cot))[which]
        block = i - t if direction == 0 else i + t
        src = own if t == 0 else land.at[block]
        to = i + 1 if direction == 0 else i - 1
        return remote(src, land.at[block], zs.at[which, direction, t], zr.at[which, direction, t], {"ch": to})

    def zsends(direction, t):
        return (i < n - 1) & (i - t >= 0) if direction == 0 else (i > 0) & (i + t <= n - 1)

    def zrecvs(direction, t):
        return i - 1 - t >= 0 if direction == 0 else i + 1 + t <= n - 1

    def zstart(which, t):
        for direction in range(2):
            @pl.when(zsends(direction, t))
            def _():
                zcopy(which, direction, t).start()

    def zwait(which, t):
        land = (lv, lc)[which]
        for direction in range(2):
            @pl.when(zrecvs(direction, t))
            def _():
                spot = land.at[i - 1 - t if direction == 0 else i + 1 + t]
                remote(spot, spot, zs.at[which, direction, t], zr.at[which, direction, t], {"ch": (i + 1) % n}).wait_recv()

    def zshift(which, t):
        land, buf = ((lv, vall), (lc, call))[which]
        size = land.shape[1]
        for direction in range(2):
            @pl.when(zrecvs(direction, t))
            def _():
                block = i - 1 - t if direction == 0 else i + 1 + t
                place = rows(block, size)
                x = land[block]
                before, after = shifts(x, W)
                buf[0, place, :] = before if which == 0 else after
                buf[1, place, :] = x
                buf[2, place, :] = after if which == 0 else before

    def zfinish(which, t):
        for direction in range(2):
            @pl.when(zsends(direction, t))
            def _():
                zcopy(which, direction, t).wait_send()

    def crim_copy(up):
        plane = cot.at[:, (D - 1) * HW : D * HW] if up else cot.at[:, 0:HW]
        k = 0 if up else 1
        return remote(plane, crim.at[k], cs.at[k], cr.at[k], {"sp": s + 1 if up else s - 1})

    def rim_copy(which, up):
        acc, buf = ((racc, rbuf), (iacc, ibuf))[which]
        k = 0 if up else 1
        src = acc.at[D + 1 if up else 0, :, W : W + HW]
        return remote(src, buf.at[k], rims.at[which, k], rimr.at[which, k], {"sp": s + 1 if up else s - 1})

    def both_ways(act):
        @pl.when(s < S - 1)
        def _():
            act(True)

        @pl.when(s > 0)
        def _():
            act(False)

    carried = -(-G // S)

    def w1_copy(r, d):
        g = s + r * S
        return remote(
            swb.at[r, (i + d) % n], wsb.at[g, rows(i, fb), :], ws1.at[r, d - 1], wr1.at[r, d - 1], {"ch": (i + d) % n}
        )

    def w2_copy(r, d, g):
        to = ((m + d) % half) * 2 + e
        return remote(wsb.at[g], wsb.at[g], ws2.at[r, d - 1], wr2.at[r, d - 1], {"sp": to})

    def w3_copy(r, d, g):
        return remote(wsb.at[g], wsb.at[g], ws3.at[r, d], wr3.at[r, d], {"sp": sib})

    def w_from(d, core, act):
        for r in range(carried):
            g = ((m - d + half) % half) * 2 + core + r * S

            @pl.when(g < G)
            def _():
                act(r, d, g)

    def w_mine(act):
        for r in range(carried):
            @pl.when(s + r * S < G)
            def _():
                act(r, s + r * S)

    zstart(0, 0)
    both_ways(lambda up: crim_copy(up).start())

    tpg = W // cb

    def w1_go(r, g):
        c, q = g // gpc, g % gpc
        taps = [filt[jnp.minimum(q * tpg + u, 8) * 3 + c] for u in range(tpg)]
        for j in range(n):
            swb[r, j] = jnp.concatenate([tap[:, j * cb : (j + 1) * cb] for tap in taps], axis=1)
        for d in range(1, n):
            w1_copy(r, d).start()
        wsb[g, rows(i, fb), :] = swb[r, i]

    w_mine(w1_go)

    x = vol[...]
    before, after = shifts(x, W)
    vall[0, rows(i, cb), :] = before
    vall[1, rows(i, cb), :] = x
    vall[2, rows(i, cb), :] = after
    x = cot[...]
    before, after = shifts(x, W)
    call[0, rows(i, fb), :] = after
    call[1, rows(i, fb), :] = x
    call[2, rows(i, fb), :] = before
    ends = (i == 0) | (i == n - 1)
    far = jnp.where(i == 0, n - 1, 0)

    @pl.when(ends)
    def _():
        for c in range(3):
            call[c, rows(far, fb), :] = jnp.zeros((fb, cells), BF)

    edge[...] = jnp.zeros_like(edge)
    for c, part in enumerate((after, x, before)):
        for z in range(D):
            edge[c, z + 1, :, W : W + HW] = part[:, z * HW : (z + 1) * HW]
    for k in range(9):
        for c in range(3):
            wfwd[k * fb : (k + 1) * fb, c * cb * n : (c + 1) * cb * n] = filt[3 * k + c]
    racc[...] = jnp.zeros_like(racc)
    iacc[...] = jnp.zeros_like(iacc)

    def w2_go(r, g):
        for d in range(1, n):
            w1_copy(r, d).wait()
        for d in range(1, half):
            w2_copy(r, d, g).start()
        w3_copy(r, 0, g).start()

    def early():
        @pl.when(s > 0)
        def _():
            remote(crim.at[0], crim.at[0], cs.at[0], cr.at[0], {"sp": (s + 1) % S}).wait_recv()
            x = crim[0]
            before, after = shifts(x, W)
            for c, part in enumerate((after, x, before)):
                edge[c, 0, :, W : W + HW] = part

        @pl.when(s < S - 1)
        def _():
            remote(crim.at[1], crim.at[1], cs.at[1], cr.at[1], {"sp": (s + 1) % S}).wait_recv()
            x = crim[1]
            before, after = shifts(x, W)
            for c, part in enumerate((after, x, before)):
                edge[c, D + 1, :, W : W + HW] = part

    R, Ch = fpart.shape[3], fpart.shape[4]
    pair = i // (n // 2)

    def fgrad(h):
        flat = fpart.at[h].reshape(2 * half * R, Ch)
        if 27 * fb < 2 * half * R:
            flat[27 * fb :, :] = jnp.zeros((2 * half * R - 27 * fb, Ch), F32)
        place = rows(pair if h == 0 else 1 - pair, Ch)

        def body(a, _):
            total = jnp.zeros((9 * fb, Ch), F32)
            for z in range(D):
                plane = z + 2 - a
                left = jnp.concatenate(
                    [edge[c, plane, :, (2 - b) * W : (2 - b) * W + HW] for b in range(3) for c in range(3)], axis=0
                )
                total += lax.dot_general(
                    left, vall[1, place, z * HW : (z + 1) * HW], (((1,), (1,)), ((), ())), preferred_element_type=F32
                )
            flat[rows(a, 9 * fb), :] = total
            return 0

        lax.fori_loop(0, 3, body, 0)
        f1_copy(h).start()

    def f1_copy(h):
        return remote(fpart.at[h, 1 - e], rs1.at[h], f1s.at[h], f1r.at[h], {"sp": sib})

    def f2_copy(h, d):
        to = ((m + d) % half) * 2 + e
        src = fpart.at[h, e, (m + d) % half]
        return remote(src, rs2.at[h, d - 1], f2s.at[h, d - 1], f2r.at[h, d - 1], {"sp": to})

    def reduce_pair(h):
        f1_copy(h).wait()
        fpart[h, e] = fpart[h, e] + rs1[h]
        for d in range(1, half):
            f2_copy(h, d).start()

    def a1_copy(h, d):
        spot = fog.at[h, e, m]
        return remote(spot, spot, a1s.at[h, d - 1], a1r.at[h, d - 1], {"sp": ((m + d) % half) * 2 + e})

    def a2_copy(h, d):
        spot = fog.at[h, e, (m - d + half) % half]
        return remote(spot, spot, a2s.at[h, d], a2r.at[h, d], {"sp": sib})

    def reduce_chips(h):
        total = fpart[h, e, m]
        for d in range(1, half):
            f2_copy(h, d).wait()
            total = total + rs2[h, d - 1]
        fog[h, e, m] = (total * factor).astype(BF)
        for d in range(1, half):
            a1_copy(h, d).start()
        a2_copy(h, 0).start()

    def gather_forward(h):
        for d in range(1, half):
            a1_copy(h, d).wait_recv()
            a2_copy(h, d).start()

    def gather_end(h):
        for d in range(half):
            spot = fog.at[h, 1 - e, (m - d + half) % half]
            remote(spot, spot, a2s.at[h, d], a2r.at[h, d], {"sp": sib}).wait_recv()
        lanes = pl.ds(pl.multiple_of((pair if h == 0 else 1 - pair) * Ch, Ch), Ch)
        fout[:, lanes] = fog.at[h].reshape(2 * half * R, Ch)[0 : 27 * fb, :]

    def w3_go():
        def pass_on(r, d, g):
            w2_copy(r, d, g).wait_recv()
            w3_copy(r, d, g).start()

        for d in range(1, half):
            w_from(d, e, pass_on)

    own_half = max(n // 2 - 2, 0)
    for t in range(n - 1):
        zwait(0, t)
        if t + 1 < n - 1:
            zstart(0, t + 1)
        if t + 1 == max(n - 2, 1):
            zstart(1, 0)
        zshift(0, t)
        if t == 0:
            early()
        if t == own_half:
            fgrad(0)
            w_mine(w2_go)
        if t == own_half + 1:
            reduce_pair(0)
    fgrad(1)
    w3_go()

    tile = 4 * W if H % 4 == 0 else W
    per_plane = HW // tile

    def conv(weights, pick, acc, size, forward, part):
        for z in range(D):
            rim = ([0] if z == 0 else []) + ([2] if z == D - 1 else [])
            if forward:
                rim = [2 - a for a in rim]
            taps = {"all": [0, 1, 2], "rim": rim, "rest": [a for a in range(3) if a not in rim]}[part]
            if not taps:
                continue
            low, high = min(taps), max(taps) + 1

            def body(q, _):
                lanes = pl.ds(pl.multiple_of(z * HW + q * tile, W), tile)
                right = pick(lanes)
                left = weights(pl.ds(low * 3 * size, (high - low) * 3 * size))
                product = jnp.dot(left, right, preferred_element_type=F32)
                for a in taps:
                    plane = z + 2 - a if forward else z + a
                    for b in range(3):
                        off = 2 - b if forward else b
                        spot = pl.ds(pl.multiple_of(q * tile + off * W, W), tile)
                        k = 3 * (a - low) + b
                        acc[plane, :, spot] += product[k * size : (k + 1) * size]
                return 0

            lax.fori_loop(0, per_plane, body, 0)

    def response():
        conv(
            lambda r: wfwd[r, :], lambda lanes: vall[:, :, lanes].reshape(3 * cb * n, tile), racc, fb, True, "all"
        )
        both_ways(lambda up: rim_copy(0, up).start())

    def kernel_swapped():
        for d in range(half):
            w_from(d, 1 - e, lambda r, d, g: w3_copy(r, d, g).wait_recv())

        for g in range(gpc):
            for c in range(3):
                wst[g * W : (g + 1) * W, c * F : (c + 1) * F] = wsb[c * gpc + g].T
            piece = jnp.concatenate([wsb[c * gpc + g, rows(far, fb), :] for c in range(3)], axis=0)
            wl[g * W : (g + 1) * W, :] = piece.T

    def most_blocks():
        conv(
            lambda r: wst[r, :], lambda lanes: call[:, :, lanes].reshape(3 * F, tile), iacc, cb, False, "all"
        )
        both_ways(lambda up: rim_copy(1, up).start())

    def far_rim(up):
        plane = lc.at[far, :, (D - 1) * HW : D * HW] if up else lc.at[far, :, 0:HW]
        k = 0 if up else 1
        return remote(plane, lrim.at[k], ls.at[k], lr.at[k], {"sp": s + 1 if up else s - 1})

    def far_use(k):
        remote(lrim.at[k], lrim.at[k], ls.at[k], lr.at[k], {"sp": (s + 1) % S}).wait_recv()
        x = lrim[k]
        before, after = shifts(x, W)
        right = jnp.concatenate([after, x, before], axis=0)
        a = 2 if k == 0 else 0
        product = jnp.dot(wl[3 * a * cb : 3 * (a + 1) * cb, :], right, preferred_element_type=F32)
        plane = 1 if k == 0 else D
        for b in range(3):
            iacc[plane, :, b * W : b * W + HW] += product[b * cb : (b + 1) * cb]

    def far_block():
        both_ways(lambda up: far_rim(up).start())
        x = lc[far]
        before, after = shifts(x, W)
        lcall[0:fb, :] = after
        lcall[fb : 2 * fb, :] = x
        lcall[2 * fb :, :] = before
        conv(lambda r: wl[r, :], lambda lanes: lcall[:, lanes], iacc, cb, False, "rest")

        @pl.when(s > 0)
        def _():
            far_use(0)

        @pl.when(s < S - 1)
        def _():
            far_use(1)

        both_ways(lambda up: far_rim(up).wait_send())

    def finish(which, out, acc, buf):
        @pl.when(s > 0)
        def _():
            remote(buf.at[0], buf.at[0], rims.at[which, 0], rimr.at[which, 0], {"sp": (s + 1) % S}).wait_recv()
            acc[1, :, W : W + HW] += buf[0]

        @pl.when(s < S - 1)
        def _():
            remote(buf.at[1], buf.at[1], rims.at[which, 1], rimr.at[which, 1], {"sp": (s + 1) % S}).wait_recv()
            acc[D, :, W : W + HW] += buf[1]

        for z in range(D):
            out[:, z * HW : (z + 1) * HW] = acc[z + 1, :, W : W + HW].astype(BF)

    last = n - 2
    for t in range(last):
        zwait(1, t)
        zstart(1, t + 1)
        if t == 0:
            reduce_pair(1)
            response()
            reduce_chips(0)
        zshift(1, t)
    kernel_swapped()
    reduce_chips(1)
    most_blocks()
    gather_forward(0)
    gather_forward(1)
    finish(0, resp, racc, rbuf)
    zwait(1, last)

    @pl.when(ends)
    def _():
        far_block()

    finish(1, igrad, iacc, ibuf)
    gather_end(0)
    gather_end(1)

    for which in range(2):
        for t in range(n - 1):
            zfinish(which, t)
        both_ways(lambda up: rim_copy(which, up).wait_send())
    both_ways(lambda up: crim_copy(up).wait_send())

    def w2_end(r, g):
        for d in range(1, half):
            w2_copy(r, d, g).wait_send()
        w3_copy(r, 0, g).wait_send()

    w_mine(w2_end)
    for d in range(1, half):
        w_from(d, e, lambda r, d, g: w3_copy(r, d, g).wait_send())
    for h in range(2):
        for d in range(1, half):
            a1_copy(h, d).wait_send()
        for d in range(half):
            a2_copy(h, d).wait_send()


def local(n, S, volume, filters, cotangent):
    cb, D, H, W = volume.shape
    fb = cotangent.shape[0]
    C, F = cb * n, fb * n
    cells = D * H * W
    gpc = -(-9 // (W // cb))
    G = 3 * gpc
    half = S // 2
    R = -(-27 * fb // (S * 16)) * 16
    factor = 1.0 / math.sqrt(cells * S)
    filt = jnp.transpose(filters, (1, 2, 3, 0, 4)).reshape(27, fb, C)
    dma = pltpu.SemaphoreType.DMA
    spec = pl.BlockSpec(memory_space=pltpu.VMEM)
    carried = -(-G // S)
    pads = (H + 2) * W
    resp, igrad, fgrad = pl.pallas_call(
        functools.partial(kernel, n, S, D, H, W, gpc, factor),
        out_shape=(
            jax.ShapeDtypeStruct((fb, cells), BF),
            jax.ShapeDtypeStruct((cb, cells), BF),
            jax.ShapeDtypeStruct((27 * fb, C), BF),
        ),
        in_specs=[spec] * 3,
        out_specs=(spec,) * 3,
        scratch_shapes=[
            pltpu.VMEM((3, C, cells), BF),
            pltpu.VMEM((3, F, cells), BF),
            pltpu.VMEM((3, D + 2, fb, pads), BF),
            pltpu.VMEM((2, fb, H * W), BF),
            pltpu.VMEM((D + 2, fb, pads), F32),
            pltpu.VMEM((D + 2, cb, pads), F32),
            pltpu.VMEM((2, fb, H * W), F32),
            pltpu.VMEM((2, cb, H * W), F32),
            pltpu.VMEM((9 * fb, 3 * C), BF),
            pltpu.VMEM((carried, n, fb, W), BF),
            pltpu.VMEM((G, F, W), BF),
            pltpu.VMEM((gpc * W, 3 * F), BF),
            pltpu.VMEM((gpc * W, 3 * fb), BF),
            pltpu.VMEM((n, cb, cells), BF),
            pltpu.VMEM((n, fb, cells), BF),
            pltpu.VMEM((2, fb, H * W), BF),
            pltpu.VMEM((3 * fb, cells), BF),
            pltpu.VMEM((2, 2, half, R, C // 2), F32),
            pltpu.VMEM((2, half, R, C // 2), F32),
            pltpu.VMEM((2, half - 1, R, C // 2), F32),
            pltpu.VMEM((2, 2, half, R, C // 2), BF),
            dma((2, 2, n - 1)),
            dma((2, 2, n - 1)),
            dma((carried, n - 1)),
            dma((carried, n - 1)),
            dma((carried, half - 1)),
            dma((carried, half - 1)),
            dma((2,)),
            dma((2,)),
            dma((2, 2)),
            dma((2, 2)),
            dma((2,)),
            dma((2,)),
            dma((2, half - 1)),
            dma((2, half - 1)),
            dma((2, half - 1)),
            dma((2, half - 1)),
            dma((2, half)),
            dma((2, half)),
            dma((2,)),
            dma((2,)),
            dma((carried, half)),
            dma((carried, half)),
        ],
        compiler_params=pltpu.CompilerParams(
            collective_id=0, has_side_effects=True, vmem_limit_bytes=50 * 2**20
        ),
    )(volume.reshape(cb, cells), cotangent.reshape(fb, cells), filt)
    return (
        resp.reshape(fb, D, H, W),
        igrad.reshape(cb, D, H, W),
        jnp.transpose(fgrad.reshape(3, 3, 3, fb, C), (3, 0, 1, 2, 4)),
    )


def solution(mesh):
    n, S = mesh.shape["ch"], mesh.shape["sp"]
    wide = P("ch", "sp", None, None)
    kern = P("ch", None, None, None, None)
    return jax.shard_map(
        functools.partial(local, n, S),
        mesh=mesh,
        in_specs=(wide, kern, wide),
        out_specs=(wide, wide, kern),
        check_vma=False,
    )
```

```python
import functools
import math

import jax
import jax.numpy as jnp
from jax import lax
from jax.experimental import pallas as pl
from jax.experimental.pallas import tpu as pltpu
from jax.sharding import PartitionSpec as P

BF = jnp.bfloat16
F32 = jnp.float32


def shifts(x, width):
    lane = lax.broadcasted_iota(jnp.int32, (x.shape[0], width), 1)
    first, last = lane == 0, lane == width - 1
    before, after = [], []
    for k in range(x.shape[1] // width):
        wide = x[:, k * width : (k + 1) * width].astype(F32)
        before.append(jnp.where(first, 0.0, pltpu.roll(wide, 1, 1)).astype(BF))
        after.append(jnp.where(last, 0.0, pltpu.roll(wide, width - 1, 1)).astype(BF))
    return jnp.concatenate(before, axis=1), jnp.concatenate(after, axis=1)


def kernel(
    n, S, D, H, W, gpc, factor,
    vol, cot, filt,
    resp, igrad, fout,
    vall, call, edge, crim, racc, iacc, rbuf, ibuf, wfwd, swb, wsb, wst, wl, lv, lc, lrim, lcall, fpart, rs1, rs2, fog,
    zs, zr, ws1, wr1, ws2, wr2, cs, cr, rims, rimr, f1s, f1r, f2s, f2r, a1s, a1r, a2s, a2r, ls, lr, ws3, wr3,
):
    i, s = lax.axis_index("ch"), lax.axis_index("sp")
    cb, cells = vol.shape
    fb = cot.shape[0]
    F = fb * n
    HW = H * W
    G = 3 * gpc
    half = S // 2
    m, e = s // 2, s % 2
    sib = m * 2 + 1 - e

    bar = pltpu.get_barrier_semaphore()
    for d in range(1, n):
        pl.semaphore_signal(bar, inc=1, device_id={"ch": (i + d) % n}, device_id_type=pl.DeviceIdType.MESH)
    for d in range(1, S):
        pl.semaphore_signal(bar, inc=1, device_id={"sp": (s + d) % S}, device_id_type=pl.DeviceIdType.MESH)
    pl.semaphore_wait(bar, n + S - 2)

    def remote(src, dst, ssem, rsem, dev):
        return pltpu.make_async_remote_copy(
            src_ref=src, dst_ref=dst, send_sem=ssem, recv_sem=rsem,
            device_id=dev, device_id_type=pl.DeviceIdType.MESH,
        )

    def rows(j, size):
        return pl.ds(pl.multiple_of(j * size, size), size)

    def zcopy(which, direction, t, z):
        land, own = ((lv, vol), (lc, cot))[which]
        block = i - t if direction == 0 else i + t
        src = own.at[:, z * HW : (z + 1) * HW] if t == 0 else land.at[block, z]
        to = i + 1 if direction == 0 else i - 1
        return remote(
            src, land.at[block, z], zs.at[which, direction, t, z], zr.at[which, direction, t, z], {"ch": to}
        )

    def zsends(direction, t):
        return (i < n - 1) & (i - t >= 0) if direction == 0 else (i > 0) & (i + t <= n - 1)

    def zrecvs(direction, t):
        return i - 1 - t >= 0 if direction == 0 else i + 1 + t <= n - 1

    def zstart(which, t, z):
        for direction in range(2):
            @pl.when(zsends(direction, t))
            def _():
                zcopy(which, direction, t, z).start()

    def zwait(which, t, z):
        land = (lv, lc)[which]
        for direction in range(2):
            @pl.when(zrecvs(direction, t))
            def _():
                spot = land.at[i - 1 - t if direction == 0 else i + 1 + t, z]
                remote(
                    spot, spot, zs.at[which, direction, t, z], zr.at[which, direction, t, z], {"ch": (i + 1) % n}
                ).wait_recv()

    def zshift(which, t):
        land, buf = ((lv, vall), (lc, call))[which]
        size = land.shape[2]
        for direction in range(2):
            @pl.when(zrecvs(direction, t))
            def _():
                block = i - 1 - t if direction == 0 else i + 1 + t
                place = rows(block, size)
                for z in range(D):
                    x = land[block, z]
                    before, after = shifts(x, W)
                    cells_z = slice(z * HW, (z + 1) * HW)
                    buf[0, place, cells_z] = before if which == 0 else after
                    buf[1, place, cells_z] = x
                    buf[2, place, cells_z] = after if which == 0 else before

    def zfinish(which, t):
        for direction in range(2):
            @pl.when(zsends(direction, t))
            def _():
                for z in range(D):
                    zcopy(which, direction, t, z).wait_send()

    def crim_copy(up):
        plane = cot.at[:, (D - 1) * HW : D * HW] if up else cot.at[:, 0:HW]
        k = 0 if up else 1
        return remote(plane, crim.at[k], cs.at[k], cr.at[k], {"sp": s + 1 if up else s - 1})

    def rim_copy(which, up):
        acc, buf = ((racc, rbuf), (iacc, ibuf))[which]
        k = 0 if up else 1
        src = acc.at[D + 1 if up else 0, :, W : W + HW]
        return remote(src, buf.at[k], rims.at[which, k], rimr.at[which, k], {"sp": s + 1 if up else s - 1})

    def both_ways(act):
        @pl.when(s < S - 1)
        def _():
            act(True)

        @pl.when(s > 0)
        def _():
            act(False)

    carried = -(-G // S)

    def w1_copy(r, d):
        g = s + r * S
        return remote(
            swb.at[r, (i + d) % n], wsb.at[g, rows(i, fb), :], ws1.at[r, d - 1], wr1.at[r, d - 1], {"ch": (i + d) % n}
        )

    def w2_copy(r, d, g):
        to = ((m + d) % half) * 2 + e
        return remote(wsb.at[g], wsb.at[g], ws2.at[r, d - 1], wr2.at[r, d - 1], {"sp": to})

    def w3_copy(r, d, g):
        return remote(wsb.at[g], wsb.at[g], ws3.at[r, d], wr3.at[r, d], {"sp": sib})

    def w_from(d, core, act):
        for r in range(carried):
            g = ((m - d + half) % half) * 2 + core + r * S

            @pl.when(g < G)
            def _():
                act(r, d, g)

    def w_mine(act):
        for r in range(carried):
            @pl.when(s + r * S < G)
            def _():
                act(r, s + r * S)

    for z in range(D):
        zstart(0, 0, z)
    both_ways(lambda up: crim_copy(up).start())

    tpg = W // cb

    def w1_go(r, g):
        c, q = g // gpc, g % gpc
        taps = [filt[jnp.minimum(q * tpg + u, 8) * 3 + c] for u in range(tpg)]
        for j in range(n):
            swb[r, j] = jnp.concatenate([tap[:, j * cb : (j + 1) * cb] for tap in taps], axis=1)
        for d in range(1, n):
            w1_copy(r, d).start()
        wsb[g, rows(i, fb), :] = swb[r, i]

    w_mine(w1_go)

    x = vol[...]
    before, after = shifts(x, W)
    vall[0, rows(i, cb), :] = before
    vall[1, rows(i, cb), :] = x
    vall[2, rows(i, cb), :] = after
    x = cot[...]
    before, after = shifts(x, W)
    call[0, rows(i, fb), :] = after
    call[1, rows(i, fb), :] = x
    call[2, rows(i, fb), :] = before
    ends = (i == 0) | (i == n - 1)
    far = jnp.where(i == 0, n - 1, 0)

    @pl.when(ends)
    def _():
        for c in range(3):
            call[c, rows(far, fb), :] = jnp.zeros((fb, cells), BF)

    edge[...] = jnp.zeros_like(edge)
    for c, part in enumerate((after, x, before)):
        for z in range(D):
            edge[c, z + 1, :, W : W + HW] = part[:, z * HW : (z + 1) * HW]
    for k in range(9):
        for c in range(3):
            wfwd[k * fb : (k + 1) * fb, c * cb * n : (c + 1) * cb * n] = filt[3 * k + c]
    racc[...] = jnp.zeros_like(racc)
    iacc[...] = jnp.zeros_like(iacc)

    def w2_go(r, g):
        for d in range(1, n):
            w1_copy(r, d).wait()
        for d in range(1, half):
            w2_copy(r, d, g).start()
        w3_copy(r, 0, g).start()

    def early():
        @pl.when(s > 0)
        def _():
            remote(crim.at[0], crim.at[0], cs.at[0], cr.at[0], {"sp": (s + 1) % S}).wait_recv()
            x = crim[0]
            before, after = shifts(x, W)
            for c, part in enumerate((after, x, before)):
                edge[c, 0, :, W : W + HW] = part

        @pl.when(s < S - 1)
        def _():
            remote(crim.at[1], crim.at[1], cs.at[1], cr.at[1], {"sp": (s + 1) % S}).wait_recv()
            x = crim[1]
            before, after = shifts(x, W)
            for c, part in enumerate((after, x, before)):
                edge[c, D + 1, :, W : W + HW] = part

    R, Ch = fpart.shape[3], fpart.shape[4]
    pair = i // (n // 2)

    def fgrad(h):
        flat = fpart.at[h].reshape(2 * half * R, Ch)
        if 27 * fb < 2 * half * R:
            flat[27 * fb :, :] = jnp.zeros((2 * half * R - 27 * fb, Ch), F32)
        place = rows(pair if h == 0 else 1 - pair, Ch)

        def body(a, _):
            total = jnp.zeros((9 * fb, Ch), F32)
            for z in range(D):
                plane = z + 2 - a
                left = jnp.concatenate(
                    [edge[c, plane, :, (2 - b) * W : (2 - b) * W + HW] for b in range(3) for c in range(3)], axis=0
                )
                total += lax.dot_general(
                    left, vall[1, place, z * HW : (z + 1) * HW], (((1,), (1,)), ((), ())), preferred_element_type=F32
                )
            flat[rows(a, 9 * fb), :] = total
            return 0

        lax.fori_loop(0, 3, body, 0)
        f1_copy(h).start()

    def f1_copy(h):
        return remote(fpart.at[h, 1 - e], rs1.at[h], f1s.at[h], f1r.at[h], {"sp": sib})

    def f2_copy(h, d):
        to = ((m + d) % half) * 2 + e
        src = fpart.at[h, e, (m + d) % half]
        return remote(src, rs2.at[h, d - 1], f2s.at[h, d - 1], f2r.at[h, d - 1], {"sp": to})

    def reduce_pair(h):
        f1_copy(h).wait()
        fpart[h, e] = fpart[h, e] + rs1[h]
        for d in range(1, half):
            f2_copy(h, d).start()

    def a1_copy(h, d):
        spot = fog.at[h, e, m]
        return remote(spot, spot, a1s.at[h, d - 1], a1r.at[h, d - 1], {"sp": ((m + d) % half) * 2 + e})

    def a2_copy(h, d):
        spot = fog.at[h, e, (m - d + half) % half]
        return remote(spot, spot, a2s.at[h, d], a2r.at[h, d], {"sp": sib})

    def reduce_chips(h):
        total = fpart[h, e, m]
        for d in range(1, half):
            f2_copy(h, d).wait()
            total = total + rs2[h, d - 1]
        fog[h, e, m] = (total * factor).astype(BF)
        for d in range(1, half):
            a1_copy(h, d).start()
        a2_copy(h, 0).start()

    def gather_forward(h):
        for d in range(1, half):
            a1_copy(h, d).wait_recv()
            a2_copy(h, d).start()

    def gather_end(h):
        for d in range(half):
            spot = fog.at[h, 1 - e, (m - d + half) % half]
            remote(spot, spot, a2s.at[h, d], a2r.at[h, d], {"sp": sib}).wait_recv()
        lanes = pl.ds(pl.multiple_of((pair if h == 0 else 1 - pair) * Ch, Ch), Ch)
        fout[:, lanes] = fog.at[h].reshape(2 * half * R, Ch)[0 : 27 * fb, :]

    def w3_go():
        def pass_on(r, d, g):
            w2_copy(r, d, g).wait_recv()
            w3_copy(r, d, g).start()

        for d in range(1, half):
            w_from(d, e, pass_on)

    own_half = max(n // 2 - 2, 0)
    for t in range(n - 1):
        for z in range(D):
            zwait(0, t, z)
            if t + 1 < n - 1:
                zstart(0, t + 1, z)
        if t + 1 == max(n - 2, 1):
            for z in range(D):
                zstart(1, 0, z)
        if t == own_half + 1:
            @pl.when(jnp.logical_not(ends))
            def _():
                fgrad(0)

        zshift(0, t)
        if t == 0:
            early()
        if t == own_half:
            @pl.when(ends)
            def _():
                fgrad(0)

            w_mine(w2_go)
        if t == own_half + 1:
            reduce_pair(0)
    fgrad(1)
    w3_go()

    tile = 4 * W if H % 4 == 0 else W
    per_plane = HW // tile

    def conv(weights, pick, acc, size, forward, part, planes=range(D)):
        for z in planes:
            rim = ([0] if z == 0 else []) + ([2] if z == D - 1 else [])
            if forward:
                rim = [2 - a for a in rim]
            taps = {"all": [0, 1, 2], "rim": rim, "rest": [a for a in range(3) if a not in rim]}[part]
            if not taps:
                continue
            low, high = min(taps), max(taps) + 1

            def body(q, _):
                lanes = pl.ds(pl.multiple_of(z * HW + q * tile, W), tile)
                right = pick(lanes)
                left = weights(pl.ds(low * 3 * size, (high - low) * 3 * size))
                product = jnp.dot(left, right, preferred_element_type=F32)
                for a in taps:
                    plane = z + 2 - a if forward else z + a
                    for b in range(3):
                        off = 2 - b if forward else b
                        spot = pl.ds(pl.multiple_of(q * tile + off * W, W), tile)
                        k = 3 * (a - low) + b
                        acc[plane, :, spot] += product[k * size : (k + 1) * size]
                return 0

            lax.fori_loop(0, per_plane, body, 0)

    def response():
        conv(
            lambda r: wfwd[r, :], lambda lanes: vall[:, :, lanes].reshape(3 * cb * n, tile), racc, fb, True, "all"
        )
        both_ways(lambda up: rim_copy(0, up).start())

    def kernel_swapped():
        for d in range(half):
            w_from(d, 1 - e, lambda r, d, g: w3_copy(r, d, g).wait_recv())

        for g in range(gpc):
            for c in range(3):
                wst[g * W : (g + 1) * W, c * F : (c + 1) * F] = wsb[c * gpc + g].T
            piece = jnp.concatenate([wsb[c * gpc + g, rows(far, fb), :] for c in range(3)], axis=0)
            wl[g * W : (g + 1) * W, :] = piece.T

    def most_blocks():
        conv(
            lambda r: wst[r, :], lambda lanes: call[:, :, lanes].reshape(3 * F, tile), iacc, cb, False, "all"
        )
        both_ways(lambda up: rim_copy(1, up).start())

    def far_rim(up):
        plane = lc.at[far, D - 1 if up else 0]
        k = 0 if up else 1
        return remote(plane, lrim.at[k], ls.at[k], lr.at[k], {"sp": s + 1 if up else s - 1})

    def far_use(k):
        remote(lrim.at[k], lrim.at[k], ls.at[k], lr.at[k], {"sp": (s + 1) % S}).wait_recv()
        x = lrim[k]
        before, after = shifts(x, W)
        right = jnp.concatenate([after, x, before], axis=0)
        a = 2 if k == 0 else 0
        product = jnp.dot(wl[3 * a * cb : 3 * (a + 1) * cb, :], right, preferred_element_type=F32)
        plane = 1 if k == 0 else D
        for b in range(3):
            iacc[plane, :, b * W : b * W + HW] += product[b * cb : (b + 1) * cb]

    def far_block():
        for z in range(D):
            zwait(1, last, z)
            if z == 0:
                @pl.when(s > 0)
                def _():
                    far_rim(False).start()

            if z == D - 1:
                @pl.when(s < S - 1)
                def _():
                    far_rim(True).start()

            x = lc[far, z]
            before, after = shifts(x, W)
            for c, value in enumerate((after, x, before)):
                lcall[c * fb : (c + 1) * fb, z * HW : (z + 1) * HW] = value
            conv(lambda r: wl[r, :], lambda lanes: lcall[:, lanes], iacc, cb, False, "rest", [z])

        @pl.when(s < S - 1)
        def _():
            far_use(1)

        @pl.when(s > 0)
        def _():
            far_use(0)

        both_ways(lambda up: far_rim(up).wait_send())

    def finish(which, out, acc, buf):
        @pl.when(s > 0)
        def _():
            remote(buf.at[0], buf.at[0], rims.at[which, 0], rimr.at[which, 0], {"sp": (s + 1) % S}).wait_recv()
            acc[1, :, W : W + HW] += buf[0]

        @pl.when(s < S - 1)
        def _():
            remote(buf.at[1], buf.at[1], rims.at[which, 1], rimr.at[which, 1], {"sp": (s + 1) % S}).wait_recv()
            acc[D, :, W : W + HW] += buf[1]

        for z in range(D):
            out[:, z * HW : (z + 1) * HW] = acc[z + 1, :, W : W + HW].astype(BF)

    last = n - 2
    def forwards(t):
        @pl.when(jnp.logical_not(ends))
        def _():
            for z in range(D):
                zwait(1, t, z)
                zstart(1, t + 1, z)

    for t in range(last):
        forwards(t)
        if t == 0:
            reduce_pair(1)
    response()
    reduce_chips(0)
    for t in range(last):
        @pl.when(ends)
        def _():
            for z in range(D):
                zwait(1, t, z)

        zshift(1, t)
    kernel_swapped()
    reduce_chips(1)
    most_blocks()
    gather_forward(0)
    gather_forward(1)
    finish(0, resp, racc, rbuf)

    @pl.when(ends)
    def _():
        far_block()

    finish(1, igrad, iacc, ibuf)
    gather_end(0)
    gather_end(1)

    for which in range(2):
        for t in range(n - 1):
            zfinish(which, t)
        both_ways(lambda up: rim_copy(which, up).wait_send())
    both_ways(lambda up: crim_copy(up).wait_send())

    def w2_end(r, g):
        for d in range(1, half):
            w2_copy(r, d, g).wait_send()
        w3_copy(r, 0, g).wait_send()

    w_mine(w2_end)
    for d in range(1, half):
        w_from(d, e, lambda r, d, g: w3_copy(r, d, g).wait_send())
    for h in range(2):
        for d in range(1, half):
            a1_copy(h, d).wait_send()
        for d in range(half):
            a2_copy(h, d).wait_send()


def local(n, S, volume, filters, cotangent):
    cb, D, H, W = volume.shape
    fb = cotangent.shape[0]
    C, F = cb * n, fb * n
    cells = D * H * W
    gpc = -(-9 // (W // cb))
    G = 3 * gpc
    half = S // 2
    R = -(-27 * fb // (S * 16)) * 16
    factor = 1.0 / math.sqrt(cells * S)
    filt = jnp.transpose(filters, (1, 2, 3, 0, 4)).reshape(27, fb, C)
    dma = pltpu.SemaphoreType.DMA
    spec = pl.BlockSpec(memory_space=pltpu.VMEM)
    carried = -(-G // S)
    pads = (H + 2) * W
    resp, igrad, fgrad = pl.pallas_call(
        functools.partial(kernel, n, S, D, H, W, gpc, factor),
        out_shape=(
            jax.ShapeDtypeStruct((fb, cells), BF),
            jax.ShapeDtypeStruct((cb, cells), BF),
            jax.ShapeDtypeStruct((27 * fb, C), BF),
        ),
        in_specs=[spec] * 3,
        out_specs=(spec,) * 3,
        scratch_shapes=[
            pltpu.VMEM((3, C, cells), BF),
            pltpu.VMEM((3, F, cells), BF),
            pltpu.VMEM((3, D + 2, fb, pads), BF),
            pltpu.VMEM((2, fb, H * W), BF),
            pltpu.VMEM((D + 2, fb, pads), F32),
            pltpu.VMEM((D + 2, cb, pads), F32),
            pltpu.VMEM((2, fb, H * W), F32),
            pltpu.VMEM((2, cb, H * W), F32),
            pltpu.VMEM((9 * fb, 3 * C), BF),
            pltpu.VMEM((carried, n, fb, W), BF),
            pltpu.VMEM((G, F, W), BF),
            pltpu.VMEM((gpc * W, 3 * F), BF),
            pltpu.VMEM((gpc * W, 3 * fb), BF),
            pltpu.VMEM((n, D, cb, H * W), BF),
            pltpu.VMEM((n, D, fb, H * W), BF),
            pltpu.VMEM((2, fb, H * W), BF),
            pltpu.VMEM((3 * fb, cells), BF),
            pltpu.VMEM((2, 2, half, R, C // 2), F32),
            pltpu.VMEM((2, half, R, C // 2), F32),
            pltpu.VMEM((2, half - 1, R, C // 2), F32),
            pltpu.VMEM((2, 2, half, R, C // 2), BF),
            dma((2, 2, n - 1, D)),
            dma((2, 2, n - 1, D)),
            dma((carried, n - 1)),
            dma((carried, n - 1)),
            dma((carried, half - 1)),
            dma((carried, half - 1)),
            dma((2,)),
            dma((2,)),
            dma((2, 2)),
            dma((2, 2)),
            dma((2,)),
            dma((2,)),
            dma((2, half - 1)),
            dma((2, half - 1)),
            dma((2, half - 1)),
            dma((2, half - 1)),
            dma((2, half)),
            dma((2, half)),
            dma((2,)),
            dma((2,)),
            dma((carried, half)),
            dma((carried, half)),
        ],
        compiler_params=pltpu.CompilerParams(
            collective_id=0, has_side_effects=True, vmem_limit_bytes=50 * 2**20
        ),
    )(volume.reshape(cb, cells), cotangent.reshape(fb, cells), filt)
    return (
        resp.reshape(fb, D, H, W),
        igrad.reshape(cb, D, H, W),
        jnp.transpose(fgrad.reshape(3, 3, 3, fb, C), (3, 0, 1, 2, 4)),
    )


def solution(mesh):
    n, S = mesh.shape["ch"], mesh.shape["sp"]
    wide = P("ch", "sp", None, None)
    kern = P("ch", None, None, None, None)
    return jax.shard_map(
        functools.partial(local, n, S),
        mesh=mesh,
        in_specs=(wide, kern, wide),
        out_specs=(wide, wide, kern),
        check_vma=False,
    )
```

```python
import functools
import math

import jax
import jax.numpy as jnp
from jax import lax
from jax.experimental import pallas as pl
from jax.experimental.pallas import tpu as pltpu
from jax.sharding import PartitionSpec as P

BF = jnp.bfloat16
F32 = jnp.float32


def shifts(x, width):
    lane = lax.broadcasted_iota(jnp.int32, (x.shape[0], width), 1)
    first, last = lane == 0, lane == width - 1
    before, after = [], []
    for k in range(x.shape[1] // width):
        wide = x[:, k * width : (k + 1) * width].astype(F32)
        before.append(jnp.where(first, 0.0, pltpu.roll(wide, 1, 1)).astype(BF))
        after.append(jnp.where(last, 0.0, pltpu.roll(wide, width - 1, 1)).astype(BF))
    return jnp.concatenate(before, axis=1), jnp.concatenate(after, axis=1)


def kernel(
    n, S, D, H, W, gpc, factor,
    vol, cot, filt,
    resp, igrad, fout,
    vall, call, edge, crim, racc, iacc, rbuf, wfwd, swb, wsb, wst, wl, lv, lc, lrim, lcall, fpart, rs1, rs2, fog,
    zs, zr, ws1, wr1, ws2, wr2, cs, cr, rims, rimr, f1s, f1r, f2s, f2r, a1s, a1r, a2s, a2r, ls, lr, ws3, wr3,
):
    i, s = lax.axis_index("ch"), lax.axis_index("sp")
    cb, cells = vol.shape
    fb = cot.shape[0]
    F = fb * n
    HW = H * W
    G = 3 * gpc
    half = S // 2
    m, e = s // 2, s % 2
    sib = m * 2 + 1 - e

    bar = pltpu.get_barrier_semaphore()
    for d in range(1, n):
        pl.semaphore_signal(bar, inc=1, device_id={"ch": (i + d) % n}, device_id_type=pl.DeviceIdType.MESH)
    for d in range(1, S):
        pl.semaphore_signal(bar, inc=1, device_id={"sp": (s + d) % S}, device_id_type=pl.DeviceIdType.MESH)
    pl.semaphore_wait(bar, n + S - 2)

    def remote(src, dst, ssem, rsem, dev):
        return pltpu.make_async_remote_copy(
            src_ref=src, dst_ref=dst, send_sem=ssem, recv_sem=rsem,
            device_id=dev, device_id_type=pl.DeviceIdType.MESH,
        )

    def rows(j, size):
        return pl.ds(pl.multiple_of(j * size, size), size)

    def zcopy(which, direction, t, z):
        land, own = ((lv, vol), (lc, cot))[which]
        block = i - t if direction == 0 else i + t
        src = own.at[:, z * HW : (z + 1) * HW] if t == 0 else land.at[block, z]
        to = i + 1 if direction == 0 else i - 1
        return remote(
            src, land.at[block, z], zs.at[which, direction, t, z], zr.at[which, direction, t, z], {"ch": to}
        )

    def zsends(direction, t):
        return (i < n - 1) & (i - t >= 0) if direction == 0 else (i > 0) & (i + t <= n - 1)

    def zrecvs(direction, t):
        return i - 1 - t >= 0 if direction == 0 else i + 1 + t <= n - 1

    def zstart(which, t, z):
        for direction in range(2):
            @pl.when(zsends(direction, t))
            def _():
                zcopy(which, direction, t, z).start()

    def zwait(which, t, z):
        land = (lv, lc)[which]
        for direction in range(2):
            @pl.when(zrecvs(direction, t))
            def _():
                spot = land.at[i - 1 - t if direction == 0 else i + 1 + t, z]
                remote(
                    spot, spot, zs.at[which, direction, t, z], zr.at[which, direction, t, z], {"ch": (i + 1) % n}
                ).wait_recv()

    def zshift(which, t):
        land, buf = ((lv, vall), (lc, call))[which]
        size = land.shape[2]
        for direction in range(2):
            @pl.when(zrecvs(direction, t))
            def _():
                block = i - 1 - t if direction == 0 else i + 1 + t
                place = rows(block, size)
                for z in range(D):
                    x = land[block, z]
                    before, after = shifts(x, W)
                    at = z + which
                    cells_z = slice(at * HW, (at + 1) * HW)
                    buf[0, place, cells_z] = before if which == 0 else after
                    buf[1, place, cells_z] = x
                    buf[2, place, cells_z] = after if which == 0 else before

    def zfinish(which, t):
        for direction in range(2):
            @pl.when(zsends(direction, t))
            def _():
                for z in range(D):
                    zcopy(which, direction, t, z).wait_send()

    def crim_copy(up):
        plane = cot.at[:, (D - 1) * HW : D * HW] if up else cot.at[:, 0:HW]
        k = 0 if up else 1
        return remote(plane, crim.at[k], cs.at[k], cr.at[k], {"sp": s + 1 if up else s - 1})

    def rim_copy(up):
        k = 0 if up else 1
        src = racc.at[D + 1 if up else 0, :, W : W + HW]
        return remote(src, rbuf.at[k], rims.at[k], rimr.at[k], {"sp": s + 1 if up else s - 1})

    def both_ways(act):
        @pl.when(s < S - 1)
        def _():
            act(True)

        @pl.when(s > 0)
        def _():
            act(False)

    def block_at(direction, t):
        return i - 1 - t if direction == 0 else i + 1 + t

    def brim_copy(direction, t, up):
        k = 0 if up else 1
        block = block_at(direction, t)
        return remote(
            lc.at[block, D - 1 if up else 0], lrim.at[k, block], ls.at[k, direction, t], lr.at[k, direction, t],
            {"sp": s + 1 if up else s - 1},
        )

    def brims(t, act):
        for direction in range(2):
            @pl.when(zrecvs(direction, t))
            def _():
                both_ways(lambda up: act(brim_copy(direction, t, up)))

    def brim_wait(direction, t, k):
        spot = lrim.at[k, block_at(direction, t)]
        remote(spot, spot, ls.at[k, direction, t], lr.at[k, direction, t], {"sp": (s + 1) % S}).wait_recv()

    def brims_use(t):
        for direction in range(2):
            for k in range(2):
                @pl.when(zrecvs(direction, t) & ((s > 0) if k == 0 else (s < S - 1)))
                def _():
                    brim_wait(direction, t, k)
                    block = block_at(direction, t)
                    x = lrim[k, block]
                    before, after = shifts(x, W)
                    low = 0 if k == 0 else (D + 1) * HW
                    for c, part in enumerate((after, x, before)):
                        call[c, rows(block, fb), low : low + HW] = part

    carried = -(-G // S)

    def w1_copy(r, d):
        g = s + r * S
        return remote(
            swb.at[r, (i + d) % n], wsb.at[g, rows(i, fb), :], ws1.at[r, d - 1], wr1.at[r, d - 1], {"ch": (i + d) % n}
        )

    def w2_copy(r, d, g):
        to = ((m + d) % half) * 2 + e
        return remote(wsb.at[g], wsb.at[g], ws2.at[r, d - 1], wr2.at[r, d - 1], {"sp": to})

    def w3_copy(r, d, g):
        return remote(wsb.at[g], wsb.at[g], ws3.at[r, d], wr3.at[r, d], {"sp": sib})

    def w_from(d, core, act):
        for r in range(carried):
            g = ((m - d + half) % half) * 2 + core + r * S

            @pl.when(g < G)
            def _():
                act(r, d, g)

    def w_mine(act):
        for r in range(carried):
            @pl.when(s + r * S < G)
            def _():
                act(r, s + r * S)

    for z in range(D):
        zstart(0, 0, z)
    both_ways(lambda up: crim_copy(up).start())

    tpg = W // cb

    def w1_go(r, g):
        c, q = g // gpc, g % gpc
        taps = [filt[jnp.minimum(q * tpg + u, 8) * 3 + c] for u in range(tpg)]
        for j in range(n):
            swb[r, j] = jnp.concatenate([tap[:, j * cb : (j + 1) * cb] for tap in taps], axis=1)
        for d in range(1, n):
            w1_copy(r, d).start()
        wsb[g, rows(i, fb), :] = swb[r, i]

    w_mine(w1_go)

    x = vol[...]
    before, after = shifts(x, W)
    vall[0, rows(i, cb), :] = before
    vall[1, rows(i, cb), :] = x
    vall[2, rows(i, cb), :] = after
    x = cot[...]
    before, after = shifts(x, W)
    for c, part in enumerate((after, x, before)):
        call[c, rows(i, fb), HW : (D + 1) * HW] = part
        call[c, :, 0:HW] = jnp.zeros((F, HW), BF)
        call[c, :, (D + 1) * HW :] = jnp.zeros((F, HW), BF)
    ends = (i == 0) | (i == n - 1)
    far = jnp.where(i == 0, n - 1, 0)

    @pl.when(ends)
    def _():
        for c in range(3):
            call[c, rows(far, fb), HW : (D + 1) * HW] = jnp.zeros((fb, cells), BF)

    edge[...] = jnp.zeros_like(edge)
    for c, part in enumerate((after, x, before)):
        for z in range(D):
            edge[c, z + 1, :, W : W + HW] = part[:, z * HW : (z + 1) * HW]
    for k in range(9):
        for c in range(3):
            wfwd[k * fb : (k + 1) * fb, c * cb * n : (c + 1) * cb * n] = filt[3 * k + c]
    racc[...] = jnp.zeros_like(racc)
    iacc[...] = jnp.zeros_like(iacc)

    def w2_go(r, g):
        for d in range(1, n):
            w1_copy(r, d).wait()
        for d in range(1, half):
            w2_copy(r, d, g).start()
        w3_copy(r, 0, g).start()

    def early():
        @pl.when(s > 0)
        def _():
            remote(crim.at[0], crim.at[0], cs.at[0], cr.at[0], {"sp": (s + 1) % S}).wait_recv()
            x = crim[0]
            before, after = shifts(x, W)
            for c, part in enumerate((after, x, before)):
                edge[c, 0, :, W : W + HW] = part
                call[c, rows(i, fb), 0:HW] = part

        @pl.when(s < S - 1)
        def _():
            remote(crim.at[1], crim.at[1], cs.at[1], cr.at[1], {"sp": (s + 1) % S}).wait_recv()
            x = crim[1]
            before, after = shifts(x, W)
            for c, part in enumerate((after, x, before)):
                edge[c, D + 1, :, W : W + HW] = part
                call[c, rows(i, fb), (D + 1) * HW :] = part

    R, Ch = fpart.shape[3], fpart.shape[4]
    pair = i // (n // 2)

    def fgrad(h):
        flat = fpart.at[h].reshape(2 * half * R, Ch)
        if 27 * fb < 2 * half * R:
            flat[27 * fb :, :] = jnp.zeros((2 * half * R - 27 * fb, Ch), F32)
        place = rows(pair if h == 0 else 1 - pair, Ch)

        def body(a, _):
            total = jnp.zeros((9 * fb, Ch), F32)
            for z in range(D):
                plane = z + 2 - a
                left = jnp.concatenate(
                    [edge[c, plane, :, (2 - b) * W : (2 - b) * W + HW] for b in range(3) for c in range(3)], axis=0
                )
                total += lax.dot_general(
                    left, vall[1, place, z * HW : (z + 1) * HW], (((1,), (1,)), ((), ())), preferred_element_type=F32
                )
            flat[rows(a, 9 * fb), :] = total
            return 0

        lax.fori_loop(0, 3, body, 0)
        f1_copy(h).start()

    def f1_copy(h):
        return remote(fpart.at[h, 1 - e], rs1.at[h], f1s.at[h], f1r.at[h], {"sp": sib})

    def f2_copy(h, d):
        to = ((m + d) % half) * 2 + e
        src = fpart.at[h, e, (m + d) % half]
        return remote(src, rs2.at[h, d - 1], f2s.at[h, d - 1], f2r.at[h, d - 1], {"sp": to})

    def reduce_pair(h):
        f1_copy(h).wait()
        fpart[h, e] = fpart[h, e] + rs1[h]
        for d in range(1, half):
            f2_copy(h, d).start()

    def a1_copy(h, d):
        spot = fog.at[h, e, m]
        return remote(spot, spot, a1s.at[h, d - 1], a1r.at[h, d - 1], {"sp": ((m + d) % half) * 2 + e})

    def a2_copy(h, d):
        spot = fog.at[h, e, (m - d + half) % half]
        return remote(spot, spot, a2s.at[h, d], a2r.at[h, d], {"sp": sib})

    def reduce_chips(h):
        total = fpart[h, e, m]
        for d in range(1, half):
            f2_copy(h, d).wait()
            total = total + rs2[h, d - 1]
        fog[h, e, m] = (total * factor).astype(BF)
        for d in range(1, half):
            a1_copy(h, d).start()
        a2_copy(h, 0).start()

    def gather_forward(h):
        for d in range(1, half):
            a1_copy(h, d).wait_recv()
            a2_copy(h, d).start()

    def gather_end(h):
        for d in range(half):
            spot = fog.at[h, 1 - e, (m - d + half) % half]
            remote(spot, spot, a2s.at[h, d], a2r.at[h, d], {"sp": sib}).wait_recv()
        lanes = pl.ds(pl.multiple_of((pair if h == 0 else 1 - pair) * Ch, Ch), Ch)
        fout[:, lanes] = fog.at[h].reshape(2 * half * R, Ch)[0 : 27 * fb, :]

    def w3_go():
        def pass_on(r, d, g):
            w2_copy(r, d, g).wait_recv()
            w3_copy(r, d, g).start()

        for d in range(1, half):
            w_from(d, e, pass_on)

    own_half = max(n // 2 - 2, 0)
    for t in range(n - 1):
        for z in range(D):
            zwait(0, t, z)
            if t + 1 < n - 1:
                zstart(0, t + 1, z)
        if t + 1 == max(n - 2, 1):
            for z in range(D):
                zstart(1, 0, z)
        if t == own_half + 1:
            @pl.when(jnp.logical_not(ends))
            def _():
                fgrad(0)

        zshift(0, t)
        if t == 0:
            early()
        if t == own_half:
            @pl.when(ends)
            def _():
                fgrad(0)

            w_mine(w2_go)
        if t == own_half + 1:
            reduce_pair(0)
    fgrad(1)
    w3_go()

    tile = 4 * W if H % 4 == 0 else W
    per_plane = HW // tile

    def conv(weights, pick, acc, size, taps_of, place):
        for z, taps in taps_of:
            low, high = min(taps), max(taps) + 1

            def body(q, _):
                lanes = pl.ds(pl.multiple_of(z * HW + q * tile, W), tile)
                right = pick(lanes)
                left = weights(pl.ds(low * 3 * size, (high - low) * 3 * size))
                product = jnp.dot(left, right, preferred_element_type=F32)
                for a in taps:
                    plane, flip = place(z, a)
                    for b in range(3):
                        off = 2 - b if flip else b
                        spot = pl.ds(pl.multiple_of(q * tile + off * W, W), tile)
                        k = 3 * (a - low) + b
                        acc[plane, :, spot] += product[k * size : (k + 1) * size]
                return 0

            lax.fori_loop(0, per_plane, body, 0)

    def data_conv(weights, pick, planes):
        taps_of = [(z, [a for a in range(3) if 0 <= z + a - 2 < D]) for z in planes]
        conv(weights, pick, iacc, cb, taps_of, lambda z, a: (z + a - 1, False))

    def response():
        conv(
            lambda r: wfwd[r, :], lambda lanes: vall[:, :, lanes].reshape(3 * cb * n, tile), racc, fb,
            [(z, [0, 1, 2]) for z in range(D)], lambda z, a: (z + 2 - a, True),
        )
        both_ways(lambda up: rim_copy(up).start())

    def kernel_swapped():
        for d in range(half):
            w_from(d, 1 - e, lambda r, d, g: w3_copy(r, d, g).wait_recv())

        for g in range(gpc):
            for c in range(3):
                wst[g * W : (g + 1) * W, c * F : (c + 1) * F] = wsb[c * gpc + g].T
            piece = jnp.concatenate([wsb[c * gpc + g, rows(far, fb), :] for c in range(3)], axis=0)
            wl[g * W : (g + 1) * W, :] = piece.T

    def most_blocks():
        data_conv(lambda r: wst[r, :], lambda lanes: call[:, :, lanes].reshape(3 * F, tile), range(D + 2))

    def far_shift(x, plane):
        before, after = shifts(x, W)
        for c, value in enumerate((after, x, before)):
            lcall[c * fb : (c + 1) * fb, plane * HW : (plane + 1) * HW] = value
        data_conv(lambda r: wl[r, :], lambda lanes: lcall[:, lanes], [plane])

    def far_block():
        for z in range(D):
            zwait(1, last, z)
            for up in (False, True):
                if z == (D - 1 if up else 0):
                    for direction in range(2):
                        @pl.when(zrecvs(direction, last) & ((s < S - 1) if up else (s > 0)))
                        def _():
                            brim_copy(direction, last, up).start()

            far_shift(lc[far, z], z + 1)

        for k in (1, 0):
            for direction in range(2):
                @pl.when(zrecvs(direction, last) & ((s > 0) if k == 0 else (s < S - 1)))
                def _():
                    brim_wait(direction, last, k)
                    far_shift(lrim[k, far], 0 if k == 0 else D + 1)

    def finish(out, acc):
        for z in range(D):
            out[:, z * HW : (z + 1) * HW] = acc[z + 1, :, W : W + HW].astype(BF)

    def finish_response():
        @pl.when(s > 0)
        def _():
            remote(rbuf.at[0], rbuf.at[0], rims.at[0], rimr.at[0], {"sp": (s + 1) % S}).wait_recv()
            racc[1, :, W : W + HW] += rbuf[0]

        @pl.when(s < S - 1)
        def _():
            remote(rbuf.at[1], rbuf.at[1], rims.at[1], rimr.at[1], {"sp": (s + 1) % S}).wait_recv()
            racc[D, :, W : W + HW] += rbuf[1]

        finish(resp, racc)

    last = n - 2
    def forwards(t):
        for z in range(D):
            zwait(1, t, z)
            zstart(1, t + 1, z)
        brims(t, lambda copy: copy.start())

    forwards(0)
    reduce_pair(1)
    for t in range(1, last):
        @pl.when(jnp.logical_not(ends))
        def _():
            forwards(t)

    zshift(1, 0)
    response()
    reduce_chips(0)
    for t in range(1, last):
        @pl.when(ends)
        def _():
            forwards(t)

        zshift(1, t)
    kernel_swapped()
    for t in range(last):
        brims_use(t)
    most_blocks()
    reduce_chips(1)
    gather_forward(0)
    gather_forward(1)
    finish_response()

    @pl.when(ends)
    def _():
        far_block()

    finish(igrad, iacc)
    gather_end(0)
    gather_end(1)

    for which in range(2):
        for t in range(n - 1):
            zfinish(which, t)
    both_ways(lambda up: crim_copy(up).wait_send())
    both_ways(lambda up: rim_copy(up).wait_send())
    for t in range(n - 1):
        brims(t, lambda copy: copy.wait_send())

    def w2_end(r, g):
        for d in range(1, half):
            w2_copy(r, d, g).wait_send()
        w3_copy(r, 0, g).wait_send()

    w_mine(w2_end)
    for d in range(1, half):
        w_from(d, e, lambda r, d, g: w3_copy(r, d, g).wait_send())
    for h in range(2):
        for d in range(1, half):
            a1_copy(h, d).wait_send()
        for d in range(half):
            a2_copy(h, d).wait_send()


def local(n, S, volume, filters, cotangent):
    cb, D, H, W = volume.shape
    fb = cotangent.shape[0]
    C, F = cb * n, fb * n
    cells = D * H * W
    gpc = -(-9 // (W // cb))
    G = 3 * gpc
    half = S // 2
    R = -(-27 * fb // (S * 16)) * 16
    factor = 1.0 / math.sqrt(cells * S)
    filt = jnp.transpose(filters, (1, 2, 3, 0, 4)).reshape(27, fb, C)
    dma = pltpu.SemaphoreType.DMA
    spec = pl.BlockSpec(memory_space=pltpu.VMEM)
    carried = -(-G // S)
    pads = (H + 2) * W
    resp, igrad, fgrad = pl.pallas_call(
        functools.partial(kernel, n, S, D, H, W, gpc, factor),
        out_shape=(
            jax.ShapeDtypeStruct((fb, cells), BF),
            jax.ShapeDtypeStruct((cb, cells), BF),
            jax.ShapeDtypeStruct((27 * fb, C), BF),
        ),
        in_specs=[spec] * 3,
        out_specs=(spec,) * 3,
        scratch_shapes=[
            pltpu.VMEM((3, C, cells), BF),
            pltpu.VMEM((3, F, cells + 2 * H * W), BF),
            pltpu.VMEM((3, D + 2, fb, pads), BF),
            pltpu.VMEM((2, fb, H * W), BF),
            pltpu.VMEM((D + 2, fb, pads), F32),
            pltpu.VMEM((D + 2, cb, pads), F32),
            pltpu.VMEM((2, fb, H * W), F32),
            pltpu.VMEM((9 * fb, 3 * C), BF),
            pltpu.VMEM((carried, n, fb, W), BF),
            pltpu.VMEM((G, F, W), BF),
            pltpu.VMEM((gpc * W, 3 * F), BF),
            pltpu.VMEM((gpc * W, 3 * fb), BF),
            pltpu.VMEM((n, D, cb, H * W), BF),
            pltpu.VMEM((n, D, fb, H * W), BF),
            pltpu.VMEM((2, n, fb, H * W), BF),
            pltpu.VMEM((3 * fb, cells + 2 * H * W), BF),
            pltpu.VMEM((2, 2, half, R, C // 2), F32),
            pltpu.VMEM((2, half, R, C // 2), F32),
            pltpu.VMEM((2, half - 1, R, C // 2), F32),
            pltpu.VMEM((2, 2, half, R, C // 2), BF),
            dma((2, 2, n - 1, D)),
            dma((2, 2, n - 1, D)),
            dma((carried, n - 1)),
            dma((carried, n - 1)),
            dma((carried, half - 1)),
            dma((carried, half - 1)),
            dma((2,)),
            dma((2,)),
            dma((2,)),
            dma((2,)),
            dma((2,)),
            dma((2,)),
            dma((2, half - 1)),
            dma((2, half - 1)),
            dma((2, half - 1)),
            dma((2, half - 1)),
            dma((2, half)),
            dma((2, half)),
            dma((2, 2, n - 1)),
            dma((2, 2, n - 1)),
            dma((carried, half)),
            dma((carried, half)),
        ],
        compiler_params=pltpu.CompilerParams(
            collective_id=0, has_side_effects=True, vmem_limit_bytes=50 * 2**20
        ),
    )(volume.reshape(cb, cells), cotangent.reshape(fb, cells), filt)
    return (
        resp.reshape(fb, D, H, W),
        igrad.reshape(cb, D, H, W),
        jnp.transpose(fgrad.reshape(3, 3, 3, fb, C), (3, 0, 1, 2, 4)),
    )


def solution(mesh):
    n, S = mesh.shape["ch"], mesh.shape["sp"]
    wide = P("ch", "sp", None, None)
    kern = P("ch", None, None, None, None)
    return jax.shard_map(
        functools.partial(local, n, S),
        mesh=mesh,
        in_specs=(wide, kern, wide),
        out_specs=(wide, wide, kern),
        check_vma=False,
    )
```

```python
import functools
import math

import jax
import jax.numpy as jnp
from jax import lax
from jax.experimental import pallas as pl
from jax.experimental.pallas import tpu as pltpu
from jax.sharding import PartitionSpec as P

BF = jnp.bfloat16
F32 = jnp.float32


def shifts(x, width):
    lane = lax.broadcasted_iota(jnp.int32, (x.shape[0], width), 1)
    first, last = lane == 0, lane == width - 1
    before, after = [], []
    for k in range(x.shape[1] // width):
        wide = x[:, k * width : (k + 1) * width].astype(F32)
        before.append(jnp.where(first, 0.0, pltpu.roll(wide, 1, 1)).astype(BF))
        after.append(jnp.where(last, 0.0, pltpu.roll(wide, width - 1, 1)).astype(BF))
    return jnp.concatenate(before, axis=1), jnp.concatenate(after, axis=1)


def kernel(
    n, S, D, H, W, gpc, factor,
    vol, cot, filt,
    resp, igrad, fout,
    vall, call, edge, crim, racc, iacc, rbuf, wfwd, swb, wsb, wst, wl, lv, lc, lrim, lcall, fpart, rs1, rs2, fog,
    zs, zr, ws1, wr1, ws2, wr2, cs, cr, rims, rimr, f1s, f1r, f2s, f2r, a1s, a1r, a2s, a2r, ls, lr, ws3, wr3,
):
    i, s = lax.axis_index("ch"), lax.axis_index("sp")
    cb, cells = vol.shape
    fb = cot.shape[0]
    F = fb * n
    HW = H * W
    G = 3 * gpc
    half = S // 2
    m, e = s // 2, s % 2
    sib = m * 2 + 1 - e

    bar = pltpu.get_barrier_semaphore()
    for d in range(1, n):
        pl.semaphore_signal(bar, inc=1, device_id={"ch": (i + d) % n}, device_id_type=pl.DeviceIdType.MESH)
    for d in range(1, S):
        pl.semaphore_signal(bar, inc=1, device_id={"sp": (s + d) % S}, device_id_type=pl.DeviceIdType.MESH)
    pl.semaphore_wait(bar, n + S - 2)

    def remote(src, dst, ssem, rsem, dev):
        return pltpu.make_async_remote_copy(
            src_ref=src, dst_ref=dst, send_sem=ssem, recv_sem=rsem,
            device_id=dev, device_id_type=pl.DeviceIdType.MESH,
        )

    def rows(j, size):
        return pl.ds(pl.multiple_of(j * size, size), size)

    def zcopy(which, direction, t, z):
        land, own = ((lv, vol), (lc, cot))[which]
        block = i - t if direction == 0 else i + t
        src = own.at[:, z * HW : (z + 1) * HW] if t == 0 else land.at[block, z]
        to = i + 1 if direction == 0 else i - 1
        return remote(
            src, land.at[block, z], zs.at[which, direction, t, z], zr.at[which, direction, t, z], {"ch": to}
        )

    def zsends(direction, t):
        return (i < n - 1) & (i - t >= 0) if direction == 0 else (i > 0) & (i + t <= n - 1)

    def zrecvs(direction, t):
        return i - 1 - t >= 0 if direction == 0 else i + 1 + t <= n - 1

    def zstart(which, t, z):
        for direction in range(2):
            @pl.when(zsends(direction, t))
            def _():
                zcopy(which, direction, t, z).start()

    def zwait(which, t, z):
        land = (lv, lc)[which]
        for direction in range(2):
            @pl.when(zrecvs(direction, t))
            def _():
                spot = land.at[i - 1 - t if direction == 0 else i + 1 + t, z]
                remote(
                    spot, spot, zs.at[which, direction, t, z], zr.at[which, direction, t, z], {"ch": (i + 1) % n}
                ).wait_recv()

    def zshift(which, t):
        land, buf = ((lv, vall), (lc, call))[which]
        size = land.shape[2]
        for direction in range(2):
            @pl.when(zrecvs(direction, t))
            def _():
                block = i - 1 - t if direction == 0 else i + 1 + t
                place = rows(block, size)
                for z in range(D):
                    x = land[block, z]
                    before, after = shifts(x, W)
                    at = z + which
                    cells_z = slice(at * HW, (at + 1) * HW)
                    buf[0, place, cells_z] = before if which == 0 else after
                    buf[1, place, cells_z] = x
                    buf[2, place, cells_z] = after if which == 0 else before

    def zfinish(which, t):
        for direction in range(2):
            @pl.when(zsends(direction, t))
            def _():
                for z in range(D):
                    zcopy(which, direction, t, z).wait_send()

    def crim_copy(up):
        plane = cot.at[:, (D - 1) * HW : D * HW] if up else cot.at[:, 0:HW]
        k = 0 if up else 1
        return remote(plane, crim.at[k], cs.at[k], cr.at[k], {"sp": s + 1 if up else s - 1})

    def rim_copy(up):
        k = 0 if up else 1
        src = racc.at[D + 1 if up else 0, :, W : W + HW]
        return remote(src, rbuf.at[k], rims.at[k], rimr.at[k], {"sp": s + 1 if up else s - 1})

    def both_ways(act):
        @pl.when(s < S - 1)
        def _():
            act(True)

        @pl.when(s > 0)
        def _():
            act(False)

    def block_at(direction, t):
        return i - 1 - t if direction == 0 else i + 1 + t

    def brim_copy(direction, t, up):
        k = 0 if up else 1
        block = block_at(direction, t)
        return remote(
            lc.at[block, D - 1 if up else 0], lrim.at[k, block], ls.at[k, direction, t], lr.at[k, direction, t],
            {"sp": s + 1 if up else s - 1},
        )

    def brims(t, act):
        for direction in range(2):
            @pl.when(zrecvs(direction, t))
            def _():
                both_ways(lambda up: act(brim_copy(direction, t, up)))

    def brim_wait(direction, t, k):
        spot = lrim.at[k, block_at(direction, t)]
        remote(spot, spot, ls.at[k, direction, t], lr.at[k, direction, t], {"sp": (s + 1) % S}).wait_recv()

    def brims_use(t):
        for direction in range(2):
            for k in range(2):
                @pl.when(zrecvs(direction, t) & ((s > 0) if k == 0 else (s < S - 1)))
                def _():
                    brim_wait(direction, t, k)
                    block = block_at(direction, t)
                    x = lrim[k, block]
                    before, after = shifts(x, W)
                    low = 0 if k == 0 else (D + 1) * HW
                    for c, part in enumerate((after, x, before)):
                        call[c, rows(block, fb), low : low + HW] = part

    carried = -(-G // S)

    def w1_copy(r, d):
        g = s + r * S
        return remote(
            swb.at[r, (i + d) % n], wsb.at[g, rows(i, fb), :], ws1.at[r, d - 1], wr1.at[r, d - 1], {"ch": (i + d) % n}
        )

    def w2_copy(r, d, g):
        to = ((m + d) % half) * 2 + e
        return remote(wsb.at[g], wsb.at[g], ws2.at[r, d - 1], wr2.at[r, d - 1], {"sp": to})

    def w3_copy(r, d, g):
        return remote(wsb.at[g], wsb.at[g], ws3.at[r, d], wr3.at[r, d], {"sp": sib})

    def w_from(d, core, act):
        for r in range(carried):
            g = ((m - d + half) % half) * 2 + core + r * S

            @pl.when(g < G)
            def _():
                act(r, d, g)

    def w_mine(act):
        for r in range(carried):
            @pl.when(s + r * S < G)
            def _():
                act(r, s + r * S)

    for z in range(D):
        zstart(0, 0, z)
    both_ways(lambda up: crim_copy(up).start())

    tpg = W // cb

    def w1_go(r, g):
        c, q = g // gpc, g % gpc
        taps = [filt[jnp.minimum(q * tpg + u, 8) * 3 + c] for u in range(tpg)]
        for j in range(n):
            swb[r, j] = jnp.concatenate([tap[:, j * cb : (j + 1) * cb] for tap in taps], axis=1)
        for d in range(1, n):
            w1_copy(r, d).start()
        wsb[g, rows(i, fb), :] = swb[r, i]

    w_mine(w1_go)

    x = vol[...]
    before, after = shifts(x, W)
    vall[0, rows(i, cb), :] = before
    vall[1, rows(i, cb), :] = x
    vall[2, rows(i, cb), :] = after
    x = cot[...]
    before, after = shifts(x, W)
    for c, part in enumerate((after, x, before)):
        call[c, rows(i, fb), HW : (D + 1) * HW] = part
        call[c, :, 0:HW] = jnp.zeros((F, HW), BF)
        call[c, :, (D + 1) * HW :] = jnp.zeros((F, HW), BF)
    ends = (i == 0) | (i == n - 1)
    far = jnp.where(i == 0, n - 1, 0)

    @pl.when(ends)
    def _():
        for c in range(3):
            call[c, rows(far, fb), HW : (D + 1) * HW] = jnp.zeros((fb, cells), BF)

    edge[...] = jnp.zeros_like(edge)
    for c, part in enumerate((after, x, before)):
        for z in range(D):
            edge[c, z + 1, :, W : W + HW] = part[:, z * HW : (z + 1) * HW]
    for k in range(9):
        for c in range(3):
            wfwd[k * fb : (k + 1) * fb, c * cb * n : (c + 1) * cb * n] = filt[3 * k + c]
    racc[...] = jnp.zeros_like(racc)
    iacc[...] = jnp.zeros_like(iacc)

    def w2_go(r, g):
        for d in range(1, n):
            w1_copy(r, d).wait()
        for d in range(1, half):
            w2_copy(r, d, g).start()
        w3_copy(r, 0, g).start()

    def early():
        @pl.when(s > 0)
        def _():
            remote(crim.at[0], crim.at[0], cs.at[0], cr.at[0], {"sp": (s + 1) % S}).wait_recv()
            x = crim[0]
            before, after = shifts(x, W)
            for c, part in enumerate((after, x, before)):
                edge[c, 0, :, W : W + HW] = part
                call[c, rows(i, fb), 0:HW] = part

        @pl.when(s < S - 1)
        def _():
            remote(crim.at[1], crim.at[1], cs.at[1], cr.at[1], {"sp": (s + 1) % S}).wait_recv()
            x = crim[1]
            before, after = shifts(x, W)
            for c, part in enumerate((after, x, before)):
                edge[c, D + 1, :, W : W + HW] = part
                call[c, rows(i, fb), (D + 1) * HW :] = part

    R, Ch = fpart.shape[3], fpart.shape[4]
    pair = i // (n // 2)

    def fgrad(h):
        flat = fpart.at[h].reshape(2 * half * R, Ch)
        if 27 * fb < 2 * half * R:
            flat[27 * fb :, :] = jnp.zeros((2 * half * R - 27 * fb, Ch), F32)
        place = rows(pair if h == 0 else 1 - pair, Ch)

        def body(a, _):
            total = jnp.zeros((9 * fb, Ch), F32)
            for z in range(D):
                plane = z + 2 - a
                left = jnp.concatenate(
                    [edge[c, plane, :, (2 - b) * W : (2 - b) * W + HW] for b in range(3) for c in range(3)], axis=0
                )
                total += lax.dot_general(
                    left, vall[1, place, z * HW : (z + 1) * HW], (((1,), (1,)), ((), ())), preferred_element_type=F32
                )
            flat[rows(a, 9 * fb), :] = total
            return 0

        lax.fori_loop(0, 3, body, 0)
        f1_copy(h).start()

    def f1_copy(h):
        return remote(fpart.at[h, 1 - e], rs1.at[h], f1s.at[h], f1r.at[h], {"sp": sib})

    def f2_copy(h, d):
        to = ((m + d) % half) * 2 + e
        src = fpart.at[h, e, (m + d) % half]
        return remote(src, rs2.at[h, d - 1], f2s.at[h, d - 1], f2r.at[h, d - 1], {"sp": to})

    def reduce_pair(h):
        f1_copy(h).wait()
        fpart[h, e] = fpart[h, e] + rs1[h]
        for d in range(1, half):
            f2_copy(h, d).start()

    def a1_copy(h, d):
        spot = fog.at[h, e, m]
        return remote(spot, spot, a1s.at[h, d - 1], a1r.at[h, d - 1], {"sp": ((m + d) % half) * 2 + e})

    def a2_copy(h, d):
        spot = fog.at[h, e, (m - d + half) % half]
        return remote(spot, spot, a2s.at[h, d], a2r.at[h, d], {"sp": sib})

    def reduce_chips(h):
        total = fpart[h, e, m]
        for d in range(1, half):
            f2_copy(h, d).wait()
            total = total + rs2[h, d - 1]
        fog[h, e, m] = (total * factor).astype(BF)
        for d in range(1, half):
            a1_copy(h, d).start()
        a2_copy(h, 0).start()

    def gather_forward(h):
        for d in range(1, half):
            a1_copy(h, d).wait_recv()
            a2_copy(h, d).start()

    def gather_end(h):
        for d in range(half):
            spot = fog.at[h, 1 - e, (m - d + half) % half]
            remote(spot, spot, a2s.at[h, d], a2r.at[h, d], {"sp": sib}).wait_recv()
        lanes = pl.ds(pl.multiple_of((pair if h == 0 else 1 - pair) * Ch, Ch), Ch)
        fout[:, lanes] = fog.at[h].reshape(2 * half * R, Ch)[0 : 27 * fb, :]

    def w3_go():
        def pass_on(r, d, g):
            w2_copy(r, d, g).wait_recv()
            w3_copy(r, d, g).start()

        for d in range(1, half):
            w_from(d, e, pass_on)

    own_half = max(n // 2 - 2, 0)
    for t in range(n - 1):
        for z in range(D):
            zwait(0, t, z)
            if t + 1 < n - 1:
                zstart(0, t + 1, z)
        if t + 1 == max(n - 2, 1):
            for z in range(D):
                zstart(1, 0, z)
        if t == own_half + 1:
            @pl.when(jnp.logical_not(ends))
            def _():
                fgrad(0)

        zshift(0, t)
        if t == 0:
            early()
        if t == own_half:
            @pl.when(ends)
            def _():
                fgrad(0)

            w_mine(w2_go)
        if t == own_half + 1:
            reduce_pair(0)
    fgrad(1)
    w3_go()

    tile = 4 * W if H % 4 == 0 else W
    per_plane = HW // tile

    def conv(weights, pick, acc, size, taps_of, place):
        for z, taps in taps_of:
            low, high = min(taps), max(taps) + 1

            def body(q, _):
                lanes = pl.ds(pl.multiple_of(z * HW + q * tile, W), tile)
                right = pick(lanes)
                left = weights(pl.ds(low * 3 * size, (high - low) * 3 * size))
                product = jnp.dot(left, right, preferred_element_type=F32)
                for a in taps:
                    plane, flip = place(z, a)
                    for b in range(3):
                        off = 2 - b if flip else b
                        spot = pl.ds(pl.multiple_of(q * tile + off * W, W), tile)
                        k = 3 * (a - low) + b
                        acc[plane, :, spot] += product[k * size : (k + 1) * size]
                return 0

            lax.fori_loop(0, per_plane, body, 0)

    def data_conv(weights, pick, planes):
        taps_of = [(z, [a for a in range(3) if 0 <= z + a - 2 < D]) for z in planes]
        conv(weights, pick, iacc, cb, taps_of, lambda z, a: (z + a - 1, False))

    def response():
        conv(
            lambda r: wfwd[r, :], lambda lanes: vall[:, :, lanes].reshape(3 * cb * n, tile), racc, fb,
            [(z, [0, 1, 2]) for z in range(D)], lambda z, a: (z + 2 - a, True),
        )
        both_ways(lambda up: rim_copy(up).start())

    def kernel_swapped():
        for d in range(half):
            w_from(d, 1 - e, lambda r, d, g: w3_copy(r, d, g).wait_recv())

        for g in range(gpc):
            for c in range(3):
                wst[g * W : (g + 1) * W, c * F : (c + 1) * F] = wsb[c * gpc + g].T
            piece = jnp.concatenate([wsb[c * gpc + g, rows(far, fb), :] for c in range(3)], axis=0)
            wl[g * W : (g + 1) * W, :] = piece.T

    def most_blocks():
        data_conv(lambda r: wst[r, :], lambda lanes: call[:, :, lanes].reshape(3 * F, tile), range(D + 2))

    def far_shift(x, plane):
        before, after = shifts(x, W)
        for c, value in enumerate((after, x, before)):
            lcall[c * fb : (c + 1) * fb, plane * HW : (plane + 1) * HW] = value
        data_conv(lambda r: wl[r, :], lambda lanes: lcall[:, lanes], [plane])

    def far_block():
        for z in range(D):
            zwait(1, last, z)
            for up in (False, True):
                if z == (D - 1 if up else 0):
                    for direction in range(2):
                        @pl.when(zrecvs(direction, last) & ((s < S - 1) if up else (s > 0)))
                        def _():
                            brim_copy(direction, last, up).start()

            far_shift(lc[far, z], z + 1)

        for k in (1, 0):
            for direction in range(2):
                @pl.when(zrecvs(direction, last) & ((s > 0) if k == 0 else (s < S - 1)))
                def _():
                    brim_wait(direction, last, k)
                    far_shift(lrim[k, far], 0 if k == 0 else D + 1)

    def finish(out, acc):
        for z in range(D):
            out[:, z * HW : (z + 1) * HW] = acc[z + 1, :, W : W + HW].astype(BF)

    def finish_response():
        @pl.when(s > 0)
        def _():
            remote(rbuf.at[0], rbuf.at[0], rims.at[0], rimr.at[0], {"sp": (s + 1) % S}).wait_recv()
            racc[1, :, W : W + HW] += rbuf[0]

        @pl.when(s < S - 1)
        def _():
            remote(rbuf.at[1], rbuf.at[1], rims.at[1], rimr.at[1], {"sp": (s + 1) % S}).wait_recv()
            racc[D, :, W : W + HW] += rbuf[1]

        finish(resp, racc)

    last = n - 2
    def forwards(t):
        for z in range(D):
            zwait(1, t, z)
            zstart(1, t + 1, z)
        brims(t, lambda copy: copy.start())

    forwards(0)
    reduce_pair(1)
    for t in range(1, last):
        @pl.when(jnp.logical_not(ends))
        def _():
            forwards(t)

    zshift(1, 0)
    response()
    reduce_chips(0)
    for t in range(1, last):
        @pl.when(ends)
        def _():
            forwards(t)

        zshift(1, t)
    kernel_swapped()
    reduce_chips(1)
    gather_forward(0)
    for t in range(last):
        brims_use(t)
    most_blocks()
    gather_forward(1)
    finish_response()

    @pl.when(ends)
    def _():
        far_block()

    finish(igrad, iacc)
    gather_end(0)
    gather_end(1)

    for which in range(2):
        for t in range(n - 1):
            zfinish(which, t)
    both_ways(lambda up: crim_copy(up).wait_send())
    both_ways(lambda up: rim_copy(up).wait_send())
    for t in range(n - 1):
        brims(t, lambda copy: copy.wait_send())

    def w2_end(r, g):
        for d in range(1, half):
            w2_copy(r, d, g).wait_send()
        w3_copy(r, 0, g).wait_send()

    w_mine(w2_end)
    for d in range(1, half):
        w_from(d, e, lambda r, d, g: w3_copy(r, d, g).wait_send())
    for h in range(2):
        for d in range(1, half):
            a1_copy(h, d).wait_send()
        for d in range(half):
            a2_copy(h, d).wait_send()


def local(n, S, volume, filters, cotangent):
    cb, D, H, W = volume.shape
    fb = cotangent.shape[0]
    C, F = cb * n, fb * n
    cells = D * H * W
    gpc = -(-9 // (W // cb))
    G = 3 * gpc
    half = S // 2
    R = -(-27 * fb // (S * 16)) * 16
    factor = 1.0 / math.sqrt(cells * S)
    filt = jnp.transpose(filters, (1, 2, 3, 0, 4)).reshape(27, fb, C)
    dma = pltpu.SemaphoreType.DMA
    spec = pl.BlockSpec(memory_space=pltpu.VMEM)
    carried = -(-G // S)
    pads = (H + 2) * W
    resp, igrad, fgrad = pl.pallas_call(
        functools.partial(kernel, n, S, D, H, W, gpc, factor),
        out_shape=(
            jax.ShapeDtypeStruct((fb, cells), BF),
            jax.ShapeDtypeStruct((cb, cells), BF),
            jax.ShapeDtypeStruct((27 * fb, C), BF),
        ),
        in_specs=[spec] * 3,
        out_specs=(spec,) * 3,
        scratch_shapes=[
            pltpu.VMEM((3, C, cells), BF),
            pltpu.VMEM((3, F, cells + 2 * H * W), BF),
            pltpu.VMEM((3, D + 2, fb, pads), BF),
            pltpu.VMEM((2, fb, H * W), BF),
            pltpu.VMEM((D + 2, fb, pads), F32),
            pltpu.VMEM((D + 2, cb, pads), F32),
            pltpu.VMEM((2, fb, H * W), F32),
            pltpu.VMEM((9 * fb, 3 * C), BF),
            pltpu.VMEM((carried, n, fb, W), BF),
            pltpu.VMEM((G, F, W), BF),
            pltpu.VMEM((gpc * W, 3 * F), BF),
            pltpu.VMEM((gpc * W, 3 * fb), BF),
            pltpu.VMEM((n, D, cb, H * W), BF),
            pltpu.VMEM((n, D, fb, H * W), BF),
            pltpu.VMEM((2, n, fb, H * W), BF),
            pltpu.VMEM((3 * fb, cells + 2 * H * W), BF),
            pltpu.VMEM((2, 2, half, R, C // 2), F32),
            pltpu.VMEM((2, half, R, C // 2), F32),
            pltpu.VMEM((2, half - 1, R, C // 2), F32),
            pltpu.VMEM((2, 2, half, R, C // 2), BF),
            dma((2, 2, n - 1, D)),
            dma((2, 2, n - 1, D)),
            dma((carried, n - 1)),
            dma((carried, n - 1)),
            dma((carried, half - 1)),
            dma((carried, half - 1)),
            dma((2,)),
            dma((2,)),
            dma((2,)),
            dma((2,)),
            dma((2,)),
            dma((2,)),
            dma((2, half - 1)),
            dma((2, half - 1)),
            dma((2, half - 1)),
            dma((2, half - 1)),
            dma((2, half)),
            dma((2, half)),
            dma((2, 2, n - 1)),
            dma((2, 2, n - 1)),
            dma((carried, half)),
            dma((carried, half)),
        ],
        compiler_params=pltpu.CompilerParams(
            collective_id=0, has_side_effects=True, vmem_limit_bytes=50 * 2**20
        ),
    )(volume.reshape(cb, cells), cotangent.reshape(fb, cells), filt)
    return (
        resp.reshape(fb, D, H, W),
        igrad.reshape(cb, D, H, W),
        jnp.transpose(fgrad.reshape(3, 3, 3, fb, C), (3, 0, 1, 2, 4)),
    )


def solution(mesh):
    n, S = mesh.shape["ch"], mesh.shape["sp"]
    wide = P("ch", "sp", None, None)
    kern = P("ch", None, None, None, None)
    return jax.shard_map(
        functools.partial(local, n, S),
        mesh=mesh,
        in_specs=(wide, kern, wide),
        out_specs=(wide, wide, kern),
        check_vma=False,
    )
```
